128 devices in a mesh: lon: 8 (over y, x_hi), lat: 16 (over x_lo, z, core).
Axes of the slice: x: 4 (x_hi: 2, x_lo: 2; x = x_hi * 2 + x_lo), y: 4, z: 4, core: 2. Of those that a mesh axis runs over, the one named last changes fastest.
Arguments:
- field: float32 [8, 96, 384, 192], P(None, 'lat', 'lon'), may hold values from -6 to 6
- w_qkv: bfloat16 [192, 576], replicated, may hold values from -0.4375 to 0.4375
- w_proj: bfloat16 [192, 192], replicated, may hold values from -0.4375 to 0.4375
- w_up: bfloat16 [192, 768], replicated, may hold values from -0.4375 to 0.4375
- w_down: bfloat16 [768, 192], replicated, may hold values from -0.21875 to 0.21875
- bias_table: bfloat16 [64, 6, 3312], replicated, may hold values from -6 to 304
- window_type: int32 [4, 16], P(None, 'lat'), may hold values from 0 to 63
- region_id: int32 [8, 96], P(None, 'lat'), may hold values from 0 to 2
Outputs:
- result: float32 [8, 96, 384, 192], P(None, 'lat', 'lon')
The draws below stay inside these ranges and needn't reach their ends.
All inputs are finite; a program needn't handle non-finite values.
Results may differ from the reference program's by a relative error of at most 0.0032.
Values sent between devices are 32-bit elements; how exact they have to be, the bound alone decides.
No kernel may reach another device: no remote copies, remote signals or barrier semaphores. Data moves between devices by JAX's collectives and lax.ppermute only.
A program may use at most 128 MiB of HBM per device.

```python
import jax
import jax.numpy as jnp
from jax import lax

C = 192
HEADS = 6
HIDDEN_UNITS = 768
LEV = 8
WZ = 2
WLAT = 6
WLON = 12
HEAD_DIM = 32
WIN = 144
BIAS_LEN = 3312
NLAT = 96
NLON = 384
TYPES = 64


def draw_bias_table(key, part):
    key = jax.random.fold_in(key, 7)
    key_base = jax.random.fold_in(key, 0)
    base = jnp.clip(jax.random.normal(key_base, (TYPES, HEADS, BIAS_LEN), jnp.float32), -6.0, 6.0)
    return base.astype(jnp.bfloat16)


def with_ends(drawn, stream_key, least, top_value):
    longest = drawn.shape.index(max(drawn.shape))
    spots = []
    for shift in (0, 1):
        where = [jax.random.randint(jax.random.fold_in(stream_key, axis), (), 0, length) for axis, length in enumerate(drawn.shape)]
        where[longest] = (where[longest] + shift) % drawn.shape[longest]
        spots.append(tuple(where))
    return drawn.at[spots[0]].set(least).at[spots[1]].set(top_value)


def shard_levels(rng, shape, pieces, least, top_value):
    loudness = 1.0
    for position, shards_of in pieces:
        heights = jax.random.uniform(jax.random.fold_in(jax.random.fold_in(rng, 6), position), (shards_of,), jnp.float32, least / len(pieces), top_value / len(pieces))
        loudness = loudness * jnp.repeat(jnp.exp(heights), shape[position] // shards_of).reshape((-1,) + (1,) * (len(shape) - 1 - position))
    return loudness


def bell_draw(key, dims, spread, reach, cuts=(), kind=jnp.bfloat16):
    result = jax.random.normal(key, dims, jnp.float32) * spread
    if len(cuts) > 0:
        result = shard_levels(key, dims, cuts, -0.22, 0.18) * result
    return jnp.clip(result, min=-reach, max=reach).astype(kind)


def setup_inputs(seed: int = 0) -> dict:
    key_list = jax.random.split(jax.random.key(seed), 9)
    field = bell_draw(key_list[0], (LEV, NLAT, NLON, C), 1.0, 6.0, ((1, 16), (2, 8)), jnp.float32)
    w_qkv = bell_draw(key_list[1], (C, 3 * C), C ** -0.5, 0.4375)
    w_proj = bell_draw(key_list[2], (C, C), C ** -0.5, 0.4375)
    w_up = bell_draw(key_list[3], (C, HIDDEN_UNITS), C ** -0.5, 0.4375)
    w_down = bell_draw(key_list[4], (HIDDEN_UNITS, C), HIDDEN_UNITS ** -0.5, 0.21875)
    bias_table = draw_bias_table(jax.random.fold_in(key_list[8], 71), 0)
    window_type = with_ends(jax.random.randint(key_list[6], (LEV // WZ, NLAT // WLAT), 0, TYPES), jax.random.fold_in(key_list[6], 1), 0, TYPES - 1).astype(jnp.int32)
    region_id = with_ends(jax.random.randint(key_list[7], (LEV, NLAT), 0, 3), jax.random.fold_in(key_list[7], 1), 0, 2).astype(jnp.int32)
    return dict(field=field, w_qkv=w_qkv, w_proj=w_proj, w_up=w_up, w_down=w_down, bias_table=bias_table, window_type=window_type, region_id=region_id)


def rel_index():
    tokens_all = jnp.arange(WIN, dtype=jnp.int32)
    level_pos = tokens_all // (WLAT * WLON)
    lat_pos = tokens_all // WLON % WLAT
    lon_pos = tokens_all % WLON
    span = 2 * WLON - 1
    return (lon_pos[:, None] - lon_pos[None, :] + WLON - 1 + span * (lat_pos[:, None] * WLAT + lat_pos[None, :]) + span * WLAT * WLAT * (level_pos[:, None] * WZ + level_pos[None, :])).astype(jnp.int32)

def attend_block(inputs):
    qkv_block, table_row, region_block = inputs
    width = qkv_block.shape[-1] // 3
    length = qkv_block.shape[2]
    lon_wins = length // WLON
    split = qkv_block.reshape(WZ, WLAT, lon_wins, WLON, 3, HEADS, HEAD_DIM)
    split = split.transpose(4, 2, 5, 0, 1, 3, 6).reshape(3, lon_wins, HEADS, WIN, HEAD_DIM)
    queries = split[0].astype(jnp.float32)
    keys_all = split[1].astype(jnp.float32)
    values = split[2].astype(jnp.float32)
    bias = jnp.take(table_row.astype(jnp.float32), rel_index(), axis=1)
    token_region = jnp.broadcast_to(region_block[:, :, None], (WZ, WLAT, WLON)).reshape(WIN)
    same = token_region[:, None] == token_region[None, :]
    scores = jnp.einsum('whqd,whkd->whqk', queries, keys_all) * HEAD_DIM ** (-0.5) + bias
    scores = jnp.where(same, scores, -jnp.inf)
    top = lax.optimization_barrier(jnp.max(scores, axis=-1, keepdims=True))
    expo = jnp.exp(scores - top)
    probs = (expo / lax.optimization_barrier(jnp.sum(expo, axis=-1, keepdims=True))).astype(jnp.bfloat16)
    heads_out = jnp.einsum('whqk,whkd->whqd', probs.astype(jnp.float32), values).astype(jnp.bfloat16)
    heads_out = heads_out.reshape(lon_wins, HEADS, WZ, WLAT, WLON, HEAD_DIM)
    return heads_out.transpose(2, 3, 0, 4, 1, 5).reshape(WZ, WLAT, length, width)

def windows(qkv, bias_table, window_type, region_id):
    levels, lats, lons, triple = qkv.shape
    zwins = levels // WZ
    awins = lats // WLAT
    blocks = qkv.reshape(zwins, WZ, awins, WLAT, lons, triple).transpose(0, 2, 1, 3, 4, 5)
    blocks = blocks.reshape(zwins * awins, WZ, WLAT, lons, triple)
    rows = bias_table[window_type.reshape(-1)]
    regions = region_id.reshape(zwins, WZ, awins, WLAT).transpose(0, 2, 1, 3).reshape(zwins * awins, WZ, WLAT)
    out = lax.map(attend_block, (blocks, rows, regions))
    width = triple // 3
    out = out.reshape(zwins, awins, WZ, WLAT, lons, width).transpose(0, 2, 1, 3, 4, 5)
    return out.reshape(levels, lats, lons, width)

def normalize(values):
    mean = lax.optimization_barrier(jnp.mean(values, axis=-1, keepdims=True))
    centered = values - mean
    variance = lax.optimization_barrier(jnp.mean(centered * centered, axis=-1, keepdims=True))
    return (centered * lax.rsqrt(variance + 1e-05)).astype(jnp.bfloat16)

def reference(field, w_qkv, w_proj, w_up, w_down, bias_table, window_type, region_id):
    rolled = jnp.roll(field, (-(WZ // 2), -(WLAT // 2), -(WLON // 2)), axis=(0, 1, 2))
    qkv = jnp.dot(normalize(rolled), w_qkv, preferred_element_type=jnp.float32).astype(jnp.bfloat16)
    heads_out = windows(qkv, bias_table, window_type, region_id)
    mixed = rolled + jnp.dot(heads_out, w_proj, preferred_element_type=jnp.float32)
    hidden = jax.nn.gelu(jnp.dot(normalize(mixed), w_up, preferred_element_type=jnp.float32)).astype(jnp.bfloat16)
    shifted_out = mixed + jnp.dot(hidden, w_down, preferred_element_type=jnp.float32)
    return jnp.roll(shifted_out, (WZ // 2, WLAT // 2, WLON // 2), axis=(0, 1, 2))
```

```python
import functools

import jax
import jax.numpy as jnp
import numpy as np
from jax import lax
from jax.experimental import pallas as pl
from jax.experimental.pallas import tpu as pltpu
from jax.sharding import PartitionSpec as P

C = 192
HEADS = 6
WZ = 2
WLAT = 6
WLON = 12
HALF = 6
ROWS = 3
HEAD_DIM = 32
WIN = 144
BIAS_LEN = 3312
SPAN = 2 * WLON - 1
LANES = WLAT * SPAN
QUERIES = 72
COLS = HEADS * QUERIES
LOG2E = 1.4426950408889634
MASKED = -1e30
VMEM = 60 * 1024 * 1024


def token_slots(rows):
    slot = np.zeros((rows, WLON), np.int64)
    for r in range(rows):
        for o in range(WLON):
            slot[r, o] = r * 8 + o if o < 8 else rows * 8 + (r // 2) * 8 + (r % 2) * 4 + o - 8
    return slot


def key_picker():
    slot = token_slots(12)
    out = np.zeros((2, WIN, 384), np.float32)
    for upper in range(2):
        for part in range(2):
            for lev in range(2):
                for row in range(ROWS):
                    a = row + (0 if (part == 0) == (upper == 1) else ROWS)
                    for o in range(WLON):
                        out[upper, slot[part * 6 + lev * 3 + row, o], lev * LANES + a * SPAN + 22 - o] = 1
    return out


def column_order():
    slot = token_slots(6)
    out = np.zeros((WLON * 48, COLS), np.float32)
    for o in range(WLON):
        for r in range(6):
            for h in range(HEADS):
                out[o * 48 + r * 8 + h, h * QUERIES + slot[r, o]] = 1
    return out


def head_sum():
    out = np.zeros((QUERIES, COLS), np.float32)
    for h in range(HEADS):
        for q in range(QUERIES):
            out[q, h * QUERIES + q] = 1
    return out


def grid_order():
    slot = token_slots(6)
    out = np.zeros((6 * 48, 5 * QUERIES), np.float32)
    for r in range(6):
        for col in range(48):
            win, o = (col + HALF) // WLON, (col + HALF) % WLON
            out[r * 48 + col, win * QUERIES + slot[r, o]] = 1
    return out


def head_mask():
    out = np.zeros((C, COLS), np.float32)
    for h in range(HEADS):
        out[h * HEAD_DIM : (h + 1) * HEAD_DIM, h * QUERIES : (h + 1) * QUERIES] = 1
    return out


def pack_pair(low, high):
    return (
        low[..., :128],
        high[..., :128],
        jnp.concatenate([low[..., 128:], high[..., 128:]], axis=-1),
    )


def unpack_pair(a, b, rest):
    low = jnp.concatenate([a, rest[..., :64]], axis=-1)
    high = jnp.concatenate([b, rest[..., 64:]], axis=-1)
    return low, high


def pack_kernel(core_ref, low_ref, high_ref, near_ref, far_ref, west_ref, east_ref):
    upper = core_ref[0]
    low, high = low_ref[0], high_ref[0]
    near_at = ROWS * (1 - upper)
    far_at = ROWS * upper
    for at, out in ((near_at, near_ref), (far_at, far_ref)):
        rows = pl.ds(at, ROWS)
        for k, part in enumerate(pack_pair(low_ref[0, rows], high_ref[0, rows])):
            out[0, k] = part
    for k, part in enumerate(pack_pair(low[:, :HALF], high[:, :HALF])):
        west_ref[0, k] = part
    for k, part in enumerate(pack_pair(low[:, 48 - HALF :], high[:, 48 - HALF :])):
        east_ref[0, k] = part


def pack(core, field):
    whole = lambda level: pl.BlockSpec((1, 6, 48, C), lambda w, core: (level(w), 0, 0, 0))
    strip = pl.BlockSpec((1, 3, ROWS, 48, 128), lambda w, core: (w, 0, 0, 0, 0))
    halo = pl.BlockSpec((1, 3, 6, HALF, 128), lambda w, core: (w, 0, 0, 0, 0))
    return pl.pallas_call(
        pack_kernel,
        grid_spec=pltpu.PrefetchScalarGridSpec(
            num_scalar_prefetch=1,
            grid=(4,),
            in_specs=[whole(lambda w: 2 * w + 1), whole(lambda w: lax.rem(2 * w + 2, 8))],
            out_specs=[strip, strip, halo, halo],
        ),
        out_shape=[
            jax.ShapeDtypeStruct((4, 3, ROWS, 48, 128), jnp.float32),
            jax.ShapeDtypeStruct((4, 3, ROWS, 48, 128), jnp.float32),
            jax.ShapeDtypeStruct((4, 3, 6, HALF, 128), jnp.float32),
            jax.ShapeDtypeStruct((4, 3, 6, HALF, 128), jnp.float32),
        ],
        name="pack",
    )(core, field, field)


def bias_kernel(types_ref, regions_ref, upper_ref, table_ref, picker_ref, order_ref, out_ref):
    step = pl.program_id(0)
    upper = upper_ref[step]
    row = table_ref[0].astype(jnp.float32)
    row = jnp.concatenate([row, jnp.zeros((2, BIAS_LEN), jnp.float32)], axis=0)
    pieces = []
    for zi in range(WZ):
        for ai in range(ROWS):
            halves = []
            for zj in range(WZ):
                base = (zi * WZ + zj) * WLAT * LANES
                first = row[:, base + ai * LANES : base + (ai + 1) * LANES]
                second = row[:, base + (ai + ROWS) * LANES : base + (ai + ROWS + 1) * LANES]
                halves.append(jnp.where(upper == 1, first, second))
            halves.append(jnp.zeros((8, 384 - 2 * LANES), jnp.float32))
            pieces.append(jnp.concatenate(halves, axis=1))
    entries = jnp.concatenate(pieces, axis=0)
    rolled = jnp.concatenate(
        [entries if o == WLON - 1 else pltpu.roll(entries, WLON - 1 - o, axis=1) for o in range(WLON)], axis=0
    ).astype(jnp.bfloat16)
    picked = lax.dot_general(
        picker_ref[0], rolled, (((1,), (1,)), ((), ())), preferred_element_type=jnp.float32
    ).astype(jnp.bfloat16)
    bias = jnp.dot(picked, order_ref[...], preferred_element_type=jnp.float32)

    slot = lax.broadcasted_iota(jnp.int32, (WIN, COLS), 0)
    late = slot - 96
    key_row = jnp.where(slot < 96, slot >> 3, ((late >> 3) << 1) + ((late >> 2) & 1))
    lane = lax.broadcasted_iota(jnp.int32, (8, COLS), 1)
    query = jnp.zeros_like(lane)
    for h in range(HEADS):
        query = jnp.where(lane >= h * QUERIES, lane - h * QUERIES, query)
    late = query - 48
    query_row = jnp.where(query < 48, query >> 3, ((late >> 3) << 1) + ((late >> 2) & 1))
    key_region = jnp.zeros_like(key_row)
    query_region = jnp.zeros_like(query_row)
    for r in range(12):
        key_region = jnp.where(key_row == r, regions_ref[step, r], key_region)
    for r in range(6):
        query_region = jnp.where(query_row == r, regions_ref[step, r], query_region)
    same = key_region == query_region[:1]
    out_ref[0] = jnp.where(same, bias * LOG2E, MASKED)


def expand_bias(types, regions, upper, table):
    steps = types.shape[0]
    picker = jnp.asarray(key_picker(), jnp.bfloat16)
    order = jnp.asarray(column_order(), jnp.bfloat16)
    return pl.pallas_call(
        bias_kernel,
        grid_spec=pltpu.PrefetchScalarGridSpec(
            num_scalar_prefetch=3,
            grid=(steps,),
            in_specs=[
                pl.BlockSpec((1, HEADS, BIAS_LEN), lambda s, types, regions, upper: (types[s], 0, 0)),
                pl.BlockSpec((1, WIN, 384), lambda s, types, regions, upper: (upper[s], 0, 0)),
                pl.BlockSpec((WLON * 48, COLS), lambda s, types, regions, upper: (0, 0)),
            ],
            out_specs=pl.BlockSpec((1, WIN, COLS), lambda s, types, regions, upper: (s, 0, 0)),
        ),
        out_shape=jax.ShapeDtypeStruct((steps, WIN, COLS), jnp.float32),
        compiler_params=pltpu.CompilerParams(vmem_limit_bytes=VMEM),
        name="expand_bias",
    )(types, regions, upper, table, picker, order)


def normalize(values):
    mean = jnp.mean(values, axis=-1, keepdims=True)
    centered = values - mean
    variance = jnp.mean(centered * centered, axis=-1, keepdims=True)
    return centered * lax.rsqrt(variance + 1e-05)


def halo_tile(values):
    return jnp.concatenate([values, jnp.zeros(values.shape[:-2] + (2, C), jnp.float32)], axis=-2)


def window_tokens(grid, west, east):
    row = lax.broadcasted_iota(jnp.int32, (1, 8, C), 1)
    turn = lambda v, by: pltpu.roll(v, by, axis=1)
    own = [turn(grid[:, 8 * t : 8 * t + 8], 6) for t in range(6)]
    east = turn(east, 6)
    first_six = row < 6
    tiles = [jnp.where(first_six, west, own[0])]
    tiles += [jnp.where(first_six, own[t - 1], own[t]) for t in range(1, 6)]
    tiles += [jnp.where(first_six, own[5], east), east]
    low = row < 4
    windows = []
    for i in range(5):
        base = 12 * i // 8
        first, second = tiles[base], tiles[base + 1]
        flipped = turn(second, 4)
        pairs = second.reshape(6, 2, 8, C)
        flipped_pairs = flipped.reshape(6, 2, 8, C)
        if i % 2 == 0:
            front = first
            back = jnp.where(low, pairs[:, 0], flipped_pairs[:, 1])
        else:
            front = jnp.where(low, turn(first, 4), flipped)
            back = jnp.where(low, flipped_pairs[:, 0], pairs[:, 1])
        windows.append(jnp.concatenate([front.reshape(96, C), back.reshape(48, C)], axis=0))
    return windows


def nt(a, b):
    return lax.dot_general(a, b, (((1,), (1,)), ((), ())), preferred_element_type=jnp.float32)


def half_kernel(
    at_ref, low_ref, high_ref, strip_ref, west_ref, east_ref, corner_ref, bias_ref,
    wq_ref, wk_ref, wvt_ref, wproj_ref, wup_ref, wdown_ref, heads_ref, mask_ref, order_ref, *rest,
):
    out_ref = rest[-1]
    bf = jnp.bfloat16
    own = jnp.concatenate([low_ref[0], high_ref[0]], axis=0)
    strip = jnp.concatenate(unpack_pair(*[strip_ref[0, k] for k in range(3)]), axis=0)

    def halo(at):
        return halo_tile(jnp.concatenate(unpack_pair(*[at(k) for k in range(3)]), axis=0))

    west = jnp.concatenate([halo(lambda k: west_ref[0, k]), halo(lambda k: corner_ref[0, 0, k])], axis=0)
    east = jnp.concatenate([halo(lambda k: east_ref[0, k]), halo(lambda k: corner_ref[1, 0, k])], axis=0)
    grid = normalize(jnp.concatenate([own, strip], axis=0))
    wins = window_tokens(grid, normalize(west), normalize(east))

    lane = lax.broadcasted_iota(jnp.int32, (1, C), 1) // HEAD_DIM
    outs = []
    for tokens in wins:
        mine = jnp.concatenate([tokens[:48], tokens[96:120]], axis=0).astype(bf)
        tokens = tokens.astype(bf)
        keys = jnp.dot(tokens, wk_ref[...], preferred_element_type=jnp.float32).astype(bf)
        values = nt(wvt_ref[...], tokens).astype(bf)
        queries = jnp.dot(mine, wq_ref[...], preferred_element_type=jnp.float32)
        spread = jnp.concatenate([jnp.where(lane == h, queries, 0.0) for h in range(HEADS)], axis=0).astype(bf)
        scores = nt(keys, spread) * (HEAD_DIM**-0.5 * LOG2E) + bias_ref[0]
        expo = jnp.exp2(scores - jnp.max(scores, axis=0, keepdims=True))
        probs = (expo * (1.0 / jnp.sum(expo, axis=0, keepdims=True))).astype(bf)
        mixed = jnp.dot(values, probs, preferred_element_type=jnp.float32) * mask_ref[...]
        outs.append(nt(heads_ref[...], mixed.astype(bf)))
    heads_out = jnp.concatenate(outs, axis=0).astype(bf)
    heads_out = jnp.dot(order_ref[...], heads_out, preferred_element_type=jnp.float32).astype(bf)
    mixed = own.reshape(6 * 48, C) + jnp.dot(heads_out, wproj_ref[...], preferred_element_type=jnp.float32)
    hidden = jax.nn.gelu(
        jnp.dot(normalize(mixed).astype(bf), wup_ref[...], preferred_element_type=jnp.float32)
    ).astype(bf)
    result = mixed + jnp.dot(hidden, wdown_ref[...], preferred_element_type=jnp.float32)
    result = result.reshape(2, ROWS, 48, C)
    rows = pl.ds(at_ref[0] * ROWS, ROWS)
    step = pl.program_id(0)
    out_ref[2 * step + 1] = result[0]
    out_ref[lax.rem(2 * step + 2, 8)] = result[1]


def half_block(at, field, strip, west, east, corners, bias, weights, so_far=None):
    const = lambda a: pl.BlockSpec(a.shape, lambda w, at: (0,) * a.ndim)
    level = lambda f: pl.BlockSpec((1, ROWS, 48, C), lambda w, at: (f(w), at[0], 0, 0))
    halo = pl.BlockSpec((1, 3, ROWS, HALF, 128), lambda w, at: (w, 0, at[0], 0, 0))
    in_specs = [
        level(lambda w: 2 * w + 1),
        level(lambda w: lax.rem(2 * w + 2, 8)),
        pl.BlockSpec((1, 3, ROWS, 48, 128), lambda w, at: (w, 0, 0, 0, 0)),
        halo,
        halo,
        pl.BlockSpec((2, 1, 3, ROWS, HALF, 128), lambda w, at: (0, w, 0, 0, 0, 0)),
        pl.BlockSpec((1, WIN, COLS), lambda w, at: (w, 0, 0)),
    ] + [const(a) for a in weights]
    operands = [at, field, field, strip, west, east, corners, bias, *weights]
    aliases = {}
    if so_far is not None:
        in_specs.append(pl.BlockSpec(memory_space=pl.ANY))
        operands.append(so_far)
        aliases = {len(operands) - 1: 0}
    return pl.pallas_call(
        half_kernel,
        grid_spec=pltpu.PrefetchScalarGridSpec(
            num_scalar_prefetch=1,
            grid=(4,),
            in_specs=in_specs,
            out_specs=pl.BlockSpec((8, ROWS, 48, C), lambda w, at: (0, at[0], 0, 0)),
        ),
        out_shape=jax.ShapeDtypeStruct(field.shape, jnp.float32),
        input_output_aliases=aliases,
        compiler_params=pltpu.CompilerParams(vmem_limit_bytes=VMEM),
        name="half_block",
    )(*operands)


def per_device(field, w_qkv, w_proj, w_up, w_down, bias_table, window_type, region_id):
    lats, lons = lax.axis_size("lat"), lax.axis_size("lon")
    odd = lax.rem(lax.axis_index("lat"), 2).astype(jnp.int32)
    near_route = [(i, i ^ 1) for i in range(lats)]
    far_route = [(i, (i + (1 if i % 2 else -1)) % lats) for i in range(lats)]

    meta = jnp.concatenate([window_type[:, 0], region_id.reshape(-1)])
    before = lax.ppermute(meta, "lat", [(i, (i + 1) % lats) for i in range(lats)])
    near_own, far_own, to_west, to_east = pack(odd.reshape(1), field)
    east = lax.ppermute(to_west, "lon", [(i, (i - 1) % lons) for i in range(lons)])
    west = lax.ppermute(to_east, "lon", [(i, (i + 1) % lons) for i in range(lons)])
    far = lax.ppermute(far_own, "lat", far_route)
    near = lax.ppermute(near_own, "lat", near_route)
    near_at, far_at = (1 - odd) * ROWS, odd * ROWS
    cut = lambda halo, at: lax.dynamic_slice_in_dim(halo, at, ROWS, axis=2)
    near_corners = lax.ppermute(jnp.stack([cut(west, near_at), cut(east, near_at)]), "lat", near_route)
    far_corners = lax.ppermute(jnp.stack([cut(west, far_at), cut(east, far_at)]), "lat", far_route)

    near_meta = jnp.where(odd == 0, meta, before)
    far_meta = jnp.where(odd == 0, before, meta)
    both = jnp.stack([near_meta, far_meta])
    types = both[:, :4].reshape(8)
    upper = jnp.stack([1 - odd, odd])
    region = both[:, 4:].reshape(2, 4, WZ, 2, ROWS)
    region = jnp.where(upper.reshape(2, 1, 1, 1, 1) == 1, region, region[:, :, :, ::-1])
    region = region.transpose(0, 1, 3, 2, 4).reshape(8, 12)
    bias = expand_bias(types, region, jnp.repeat(upper, 4), bias_table)

    bf = jnp.bfloat16
    weights = (
        w_qkv[:, :C], w_qkv[:, C : 2 * C], w_qkv[:, 2 * C :].T, w_proj, w_up, w_down,
        jnp.asarray(head_sum(), bf), jnp.asarray(head_mask(), jnp.float32), jnp.asarray(grid_order(), bf),
    )
    out = half_block((1 - odd).reshape(1), field, near, west, east, near_corners, bias[:4], weights)
    return half_block(odd.reshape(1), field, far, west, east, far_corners, bias[4:], weights, out)


def solution(mesh):
    in_specs = (
        P(None, "lat", "lon", None),
        P(),
        P(),
        P(),
        P(),
        P(),
        P(None, "lat"),
        P(None, "lat"),
    )
    out_specs = P(None, "lat", "lon", None)
    return jax.shard_map(
        per_device, mesh=mesh, in_specs=in_specs, out_specs=out_specs, check_vma=False
    )
```

```python
import jax
import jax.numpy as jnp
import numpy as np
from jax import lax
from jax.experimental import pallas as pl
from jax.experimental.pallas import tpu as pltpu
from jax.sharding import PartitionSpec as P

C = 192
HEADS = 6
WZ = 2
WLAT = 6
WLON = 12
HALF = 6
ROWS = 3
HEAD_DIM = 32
WIN = 144
BIAS_LEN = 3312
SPAN = 2 * WLON - 1
LANES = WLAT * SPAN
QUERIES = 72
COLS = HEADS * QUERIES
LOG2E = 1.4426950408889634
MASKED = -1e30
VMEM = 60 * 1024 * 1024


def token_slots(rows):
    slot = np.zeros((rows, WLON), np.int64)
    for r in range(rows):
        for o in range(WLON):
            slot[r, o] = r * 8 + o if o < 8 else rows * 8 + (r // 2) * 8 + (r % 2) * 4 + o - 8
    return slot


def key_picker():
    slot = token_slots(12)
    out = np.zeros((2, WIN, 384), np.float32)
    for upper in range(2):
        for part in range(2):
            for lev in range(2):
                for row in range(ROWS):
                    a = row + (0 if (part == 0) == (upper == 1) else ROWS)
                    for o in range(WLON):
                        out[upper, slot[part * 6 + lev * 3 + row, o], lev * LANES + a * SPAN + 22 - o] = 1
    return out


def column_order():
    slot = token_slots(6)
    out = np.zeros((WLON * 48, COLS), np.float32)
    for o in range(WLON):
        for r in range(6):
            for h in range(HEADS):
                out[o * 48 + r * 8 + h, h * QUERIES + slot[r, o]] = 1
    return out


def pack_pair(low, high):
    return (
        low[..., :128],
        high[..., :128],
        jnp.concatenate([low[..., 128:], high[..., 128:]], axis=-1),
    )


def unpack_pair(a, b, rest):
    low = jnp.concatenate([a, rest[..., :64]], axis=-1)
    high = jnp.concatenate([b, rest[..., 64:]], axis=-1)
    return low, high


def pack_kernel(core_ref, low_ref, high_ref, near_ref, far_ref, west_ref, east_ref):
    upper = core_ref[0]
    low, high = low_ref[0], high_ref[0]
    near_at = ROWS * (1 - upper)
    far_at = ROWS * upper
    for at, out in ((near_at, near_ref), (far_at, far_ref)):
        rows = pl.ds(at, ROWS)
        for k, part in enumerate(pack_pair(low_ref[0, rows], high_ref[0, rows])):
            out[0, k] = part
    for k, part in enumerate(pack_pair(low[:, :HALF], high[:, :HALF])):
        west_ref[0, k] = part
    for k, part in enumerate(pack_pair(low[:, 48 - HALF :], high[:, 48 - HALF :])):
        east_ref[0, k] = part


def pack(core, field):
    whole = lambda level: pl.BlockSpec((1, 6, 48, C), lambda w, core: (level(w), 0, 0, 0))
    strip = pl.BlockSpec((1, 3, ROWS, 48, 128), lambda w, core: (w, 0, 0, 0, 0))
    halo = pl.BlockSpec((1, 3, 6, HALF, 128), lambda w, core: (w, 0, 0, 0, 0))
    return pl.pallas_call(
        pack_kernel,
        grid_spec=pltpu.PrefetchScalarGridSpec(
            num_scalar_prefetch=1,
            grid=(4,),
            in_specs=[whole(lambda w: 2 * w + 1), whole(lambda w: lax.rem(2 * w + 2, 8))],
            out_specs=[strip, strip, halo, halo],
        ),
        out_shape=[
            jax.ShapeDtypeStruct((4, 3, ROWS, 48, 128), jnp.float32),
            jax.ShapeDtypeStruct((4, 3, ROWS, 48, 128), jnp.float32),
            jax.ShapeDtypeStruct((4, 3, 6, HALF, 128), jnp.float32),
            jax.ShapeDtypeStruct((4, 3, 6, HALF, 128), jnp.float32),
        ],
        cost_estimate=pl.CostEstimate(flops=3000000000, bytes_accessed=9000000, transcendentals=0),
        name="pack",
    )(core, field, field)


def bias_kernel(own_ref, before_ref, *refs):
    tables, picker_ref, order_ref, out_ref = refs[:4], refs[4], refs[5], refs[6]
    bf = jnp.bfloat16
    upper = pl.program_id(0) == 0
    pick = lambda lev, column: jnp.where(upper, own_ref[lev, column], before_ref[lev, column])
    at = lax.broadcasted_iota(jnp.int32, (8, 96), 1)
    head = lax.broadcasted_iota(jnp.int32, (8, 96), 0)
    rolled = []
    for w in range(4):
        chosen = jnp.where(at == head * 16 + (pick(w, 6) & 15), 1.0, 0.0).astype(bf)
        row = jnp.dot(chosen, tables[w][...].reshape(96, BIAS_LEN), preferred_element_type=jnp.float32)
        pieces = []
        for zi in range(WZ):
            for ai in range(ROWS):
                halves = []
                for zj in range(WZ):
                    base = (zi * WZ + zj) * WLAT * LANES
                    first = row[:, base + ai * LANES : base + (ai + 1) * LANES]
                    second = row[:, base + (ai + ROWS) * LANES : base + (ai + ROWS + 1) * LANES]
                    halves.append(jnp.where(upper, first, second))
                halves.append(jnp.zeros((8, 384 - 2 * LANES), jnp.float32))
                pieces.append(jnp.concatenate(halves, axis=1))
        entries = jnp.concatenate(pieces, axis=0)
        turned = [pltpu.roll(entries, WLON - 1 - o, axis=1) for o in range(WLON - 1)] + [entries]
        rolled.append(jnp.concatenate(turned, axis=0).astype(bf))
    picked = [nt(picker_ref[0], r).astype(bf) for r in rolled]
    bias = [jnp.dot(p, order_ref[...], preferred_element_type=jnp.float32) for p in picked]

    slot = lax.broadcasted_iota(jnp.int32, (WIN, 128), 0)
    late = slot - 96
    key_row = jnp.where(slot < 96, slot >> 3, ((late >> 3) << 1) + ((late >> 2) & 1))
    lane = lax.broadcasted_iota(jnp.int32, (8, COLS), 1)
    query = lane
    for h in range(1, HEADS):
        query = jnp.where(lane >= h * QUERIES, lane - h * QUERIES, query)
    late = query - 48
    query_row = jnp.where(query < 48, query >> 3, ((late >> 3) << 1) + ((late >> 2) & 1))
    shift = jnp.where(upper, 0, ROWS)
    for w in range(4):
        key_region = jnp.zeros_like(key_row)
        query_region = jnp.zeros_like(query_row)
        for r in range(12):
            lev, row = 2 * w + r % 6 // ROWS, r % ROWS
            region = pick(lev, row + (shift if r < 6 else ROWS - shift))
            key_region = jnp.where(key_row == r, region, key_region)
            if r < 6:
                query_region = jnp.where(query_row == r, region, query_region)
        for t in range(0, COLS, 128):
            lanes = slice(t, min(t + 128, COLS))
            width = lanes.stop - t
            same = key_region[:, :width] == query_region[:1, lanes]
            out_ref[0, w, :, lanes] = jnp.where(same, bias[w][:, lanes] * LOG2E, MASKED)


def expand_bias(own, before, table):
    picker = jnp.asarray(key_picker()[::-1], jnp.bfloat16)
    order = jnp.asarray(column_order(), jnp.bfloat16)
    table = table.transpose(1, 0, 2)

    def rows(w):
        return pl.BlockSpec(
            (HEADS, 16, BIAS_LEN),
            lambda s, own, before: (0, jnp.where(s == 0, own[w, 6], before[w, 6]) >> 4, 0),
        )

    return pl.pallas_call(
        bias_kernel,
        grid_spec=pltpu.PrefetchScalarGridSpec(
            num_scalar_prefetch=2,
            grid=(2,),
            in_specs=[rows(w) for w in range(4)]
            + [
                pl.BlockSpec((1, WIN, 384), lambda s, own, before: (s, 0, 0)),
                pl.BlockSpec((WLON * 48, COLS), lambda s, own, before: (0, 0)),
            ],
            out_specs=pl.BlockSpec((1, 4, WIN, COLS), lambda s, own, before: (s, 0, 0, 0)),
        ),
        out_shape=jax.ShapeDtypeStruct((2, 4, WIN, COLS), jnp.float32),
        compiler_params=pltpu.CompilerParams(vmem_limit_bytes=VMEM),
        cost_estimate=pl.CostEstimate(flops=8000000000, bytes_accessed=24000000, transcendentals=0),
        name="expand_bias",
    )(own, before, table, table, table, table, picker, order)


def normalize(values):
    mean = jnp.mean(values, axis=-1, keepdims=True)
    centered = values - mean
    variance = jnp.mean(centered * centered, axis=-1, keepdims=True)
    return centered * lax.rsqrt(variance + 1e-05)


def halo_tile(values):
    return jnp.concatenate([values, jnp.zeros(values.shape[:-2] + (2, C), jnp.float32)], axis=-2)


def window_tokens(grid, west, east):
    row = lax.broadcasted_iota(jnp.int32, (1, 8, C), 1)
    turn = lambda v, by: pltpu.roll(v, by, axis=1)
    own = [turn(grid[:, 8 * t : 8 * t + 8], 6) for t in range(6)]
    east = turn(east, 6)
    first_six = row < 6
    tiles = [jnp.where(first_six, west, own[0])]
    tiles += [jnp.where(first_six, own[t - 1], own[t]) for t in range(1, 6)]
    tiles += [jnp.where(first_six, own[5], east), east]
    low = row < 4
    windows = []
    for i in range(5):
        base = 12 * i // 8
        first, second = tiles[base], tiles[base + 1]
        flipped = turn(second, 4)
        pairs = second.reshape(6, 2, 8, C)
        flipped_pairs = flipped.reshape(6, 2, 8, C)
        if i % 2 == 0:
            front = first
            back = jnp.where(low, pairs[:, 0], flipped_pairs[:, 1])
        else:
            front = jnp.where(low, turn(first, 4), flipped)
            back = jnp.where(low, flipped_pairs[:, 0], pairs[:, 1])
        windows.append(jnp.concatenate([front.reshape(96, C), back.reshape(48, C)], axis=0))
    return windows


def grid_tokens(windows):
    row = lax.broadcasted_iota(jnp.int32, (1, 8, C), 1)
    turn = lambda v, by: pltpu.roll(v, by, axis=1)
    low = row < 4
    tiles = [None] * 8
    for i, tokens in enumerate(windows):
        base = 12 * i // 8
        front, back = tokens[:48].reshape(6, 8, C), tokens[48:].reshape(3, 8, C)
        flipped = turn(back, 4)
        if i % 2 == 0:
            tiles[base] = front
            tiles[base + 1] = jnp.stack([back, flipped], axis=1).reshape(6, 8, C)
        else:
            front = turn(front, 4)
            tiles[base] = jnp.where(low, tiles[base], front)
            tiles[base + 1] = jnp.where(low, front, jnp.stack([flipped, back], axis=1).reshape(6, 8, C))
    tiles = [turn(t, 2) for t in tiles]
    own = [jnp.where(row < 2, tiles[t], tiles[t + 1]) for t in range(6)]
    return jnp.concatenate(own, axis=1)


def nt(a, b):
    return lax.dot_general(a, b, (((1,), (1,)), ((), ())), preferred_element_type=jnp.float32)


def half_kernel(
    odd_ref, low_ref, high_ref, strip_ref, west_ref, east_ref, corner_ref, bias_ref,
    wqkv_ref, wproj_ref, wup_ref, wdown_ref, eye_ref, *rest,
):
    out_ref, wq_ref, wk_ref, wvt_ref = rest[-4:]
    bf = jnp.bfloat16
    step = pl.program_id(0)

    @pl.when(step == 0)
    def _():
        wq_ref[...] = wqkv_ref[:, :C]
        wk_ref[...] = wqkv_ref[:, C : 2 * C]
        wvt_ref[...] = wqkv_ref[:, 2 * C :].astype(jnp.float32).T.astype(bf)

    own = jnp.concatenate([low_ref[0], high_ref[0]], axis=0)
    strip = jnp.concatenate(unpack_pair(*[strip_ref[0, k] for k in range(3)]), axis=0)

    def halo(at):
        return halo_tile(jnp.concatenate(unpack_pair(*[at(k) for k in range(3)]), axis=0))

    west = jnp.concatenate([halo(lambda k: west_ref[0, k]), halo(lambda k: corner_ref[0, 0, k])], axis=0)
    east = jnp.concatenate([halo(lambda k: east_ref[0, k]), halo(lambda k: corner_ref[1, 0, k])], axis=0)
    grid = normalize(jnp.concatenate([own, strip], axis=0))
    wins = window_tokens(grid, normalize(west), normalize(east))

    mine = jnp.concatenate([part for t in wins for part in (t[:48], t[96:120])], axis=0).astype(bf)
    tokens = [t.astype(bf) for t in wins]
    queries = jnp.dot(mine, wq_ref[...], preferred_element_type=jnp.float32)
    keys = jnp.dot(jnp.concatenate(tokens, axis=0), wk_ref[...], preferred_element_type=jnp.float32).astype(bf)
    values = [nt(wvt_ref[...], t).astype(bf) for t in tokens]
    lane = lax.broadcasted_iota(jnp.int32, (1, C), 1) // HEAD_DIM
    spread = []
    for i in range(5):
        q = queries[i * QUERIES : (i + 1) * QUERIES]
        spread.append(jnp.concatenate([jnp.where(lane == h, q, 0.0) for h in range(HEADS)], axis=0).astype(bf))
    scores = [nt(keys[i * WIN : (i + 1) * WIN], spread[i]) for i in range(5)]
    probs = []
    for s in scores:
        s = s * (HEAD_DIM**-0.5 * LOG2E) + bias_ref[0, 0]
        expo = jnp.exp2(s - jnp.max(s, axis=0, keepdims=True))
        probs.append((expo * (1.0 / jnp.sum(expo, axis=0, keepdims=True))).astype(bf))
    mixed = [jnp.dot(v, p, preferred_element_type=jnp.float32) for v, p in zip(values, probs)]
    outs = []
    for m in mixed:
        own_head = [m[h * HEAD_DIM : (h + 1) * HEAD_DIM, h * QUERIES : (h + 1) * QUERIES] for h in range(HEADS)]
        outs.append(nt(eye_ref[...], jnp.concatenate(own_head, axis=0).astype(bf)))
    heads_out = grid_tokens(outs).reshape(6 * 48, C).astype(bf)
    mixed = own.reshape(6 * 48, C) + jnp.dot(heads_out, wproj_ref[...], preferred_element_type=jnp.float32)
    hidden = jax.nn.gelu(
        jnp.dot(normalize(mixed).astype(bf), wup_ref[...], preferred_element_type=jnp.float32)
    ).astype(bf)
    result = mixed + nt(hidden, wdown_ref[...])
    result = result.reshape(2, ROWS, 48, C)
    out_ref[2 * step + 1] = result[0]
    out_ref[lax.rem(2 * step + 2, 8)] = result[1]


def half_block(near, odd, field, strip, west, east, corners, bias, weights, so_far=None):
    const = lambda a: pl.BlockSpec(a.shape, lambda w, odd: (0,) * a.ndim)
    row_of = (lambda odd: 1 - odd[0]) if near else (lambda odd: odd[0])
    level = lambda f: pl.BlockSpec((1, ROWS, 48, C), lambda w, odd: (f(w), row_of(odd), 0, 0))
    halo = pl.BlockSpec((1, 3, ROWS, HALF, 128), lambda w, odd: (w, 0, row_of(odd), 0, 0))
    in_specs = [
        level(lambda w: 2 * w + 1),
        level(lambda w: lax.rem(2 * w + 2, 8)),
        pl.BlockSpec((1, 3, ROWS, 48, 128), lambda w, odd: (w, 0, 0, 0, 0)),
        halo,
        halo,
        pl.BlockSpec((2, 1, 3, ROWS, HALF, 128), lambda w, odd: (0, w, 0, 0, 0, 0)),
        pl.BlockSpec((1, 1, WIN, COLS), lambda w, odd: (1 - row_of(odd), w, 0, 0)),
    ] + [const(a) for a in weights]
    operands = [odd, field, field, strip, west, east, corners, bias, *weights]
    aliases = {}
    if so_far is not None:
        in_specs.append(pl.BlockSpec(memory_space=pl.ANY))
        operands.append(so_far)
        aliases = {len(operands) - 1: 0}
    return pl.pallas_call(
        half_kernel,
        grid_spec=pltpu.PrefetchScalarGridSpec(
            num_scalar_prefetch=1,
            grid=(4,),
            in_specs=in_specs,
            out_specs=pl.BlockSpec((8, ROWS, 48, C), lambda w, odd: (0, row_of(odd), 0, 0)),
            scratch_shapes=[pltpu.VMEM((C, C), jnp.bfloat16)] * 3,
        ),
        out_shape=jax.ShapeDtypeStruct(field.shape, jnp.float32),
        input_output_aliases=aliases,
        compiler_params=pltpu.CompilerParams(vmem_limit_bytes=VMEM),
        cost_estimate=pl.CostEstimate(flops=14000000000, bytes_accessed=42000000, transcendentals=0),
        name="near_half" if near else "far_half",
    )(*operands)


def per_device(field, w_qkv, w_proj, w_up, w_down, bias_table, window_type, region_id):
    lats, lons = lax.axis_size("lat"), lax.axis_size("lon")
    odd = lax.rem(lax.axis_index("lat"), 2).astype(jnp.int32)
    near_route = [(i, i ^ 1) for i in range(lats)]
    far_route = [(i, (i + (1 if i % 2 else -1)) % lats) for i in range(lats)]

    meta = jnp.concatenate([region_id, jnp.pad(window_type, ((0, 4), (0, 0)))], axis=1)
    before = lax.ppermute(meta, "lat", [(i, (i + 1) % lats) for i in range(lats)])
    near_own, far_own, to_west, to_east = pack(odd.reshape(1), field)
    east = lax.ppermute(to_west, "lon", [(i, (i - 1) % lons) for i in range(lons)])
    west = lax.ppermute(to_east, "lon", [(i, (i + 1) % lons) for i in range(lons)])
    far = lax.ppermute(far_own, "lat", far_route)
    near = lax.ppermute(near_own, "lat", near_route)
    near_at, far_at = (1 - odd) * ROWS, odd * ROWS
    cut = lambda halo, at: lax.dynamic_slice_in_dim(halo, at, ROWS, axis=2)
    bias = expand_bias(meta, before, bias_table)
    west, east, bias = lax.optimization_barrier((west, east, bias))
    near_corners = lax.ppermute(jnp.stack([cut(west, near_at), cut(east, near_at)]), "lat", near_route)
    far_corners = lax.ppermute(jnp.stack([cut(west, far_at), cut(east, far_at)]), "lat", far_route)

    weights = (
        w_qkv, w_proj, w_up, w_down.T,
        jnp.eye(QUERIES, dtype=jnp.bfloat16),
    )
    core = odd.reshape(1)
    out = half_block(True, core, field, near, west, east, near_corners, bias, weights)
    return half_block(False, core, field, far, west, east, far_corners, bias, weights, out)


def solution(mesh):
    in_specs = (
        P(None, "lat", "lon", None),
        P(),
        P(),
        P(),
        P(),
        P(),
        P(None, "lat"),
        P(None, "lat"),
    )
    out_specs = P(None, "lat", "lon", None)
    return jax.shard_map(
        per_device, mesh=mesh, in_specs=in_specs, out_specs=out_specs, check_vma=False
    )
```

```python
import functools

import jax
import jax.numpy as jnp
import numpy as np
from jax import lax
from jax.experimental import pallas as pl
from jax.experimental.pallas import tpu as pltpu
from jax.sharding import PartitionSpec as P

C = 192
HEADS = 6
WZ = 2
WLAT = 6
WLON = 12
HALF = 6
ROWS = 3
HEAD_DIM = 32
WIN = 144
BIAS_LEN = 3312
SPAN = 2 * WLON - 1
LANES = WLAT * SPAN
QUERIES = 72
COLS = HEADS * QUERIES
EDGE_SLOTS = 40
EDGE_COLS = HEADS * EDGE_SLOTS
LOG2E = 1.4426950408889634
MASKED = -1e30
VMEM_LIMIT = 24 * 1024 * 1024


def token_slots(rows):
    slot = np.zeros((rows, WLON), np.int64)
    for r in range(rows):
        for o in range(WLON):
            slot[r, o] = r * 8 + o if o < 8 else rows * 8 + (r // 2) * 8 + (r % 2) * 4 + o - 8
    return slot


def key_picker():
    slot = token_slots(12)
    out = np.zeros((2, WIN, 384), np.float32)
    for upper in range(2):
        for part in range(2):
            for lev in range(2):
                for row in range(ROWS):
                    a = row + (0 if (part == 0) == (upper == 1) else ROWS)
                    for o in range(WLON):
                        out[upper, slot[part * 6 + lev * 3 + row, o], lev * LANES + a * SPAN + 22 - o] = 1
    return out


def edge_keys():
    slot = token_slots(12)
    out = np.zeros((2, WIN, 192), np.float32)
    for edge in range(2):
        for r in range(12):
            for o in range(WLON):
                mine = (o >= HALF) == (edge == 0)
                col = o % HALF + (2 if mine and edge == 1 else 0)
                out[edge, slot[r, o], (0 if mine else 96) + r * 8 + col] = 1
    return out


def edge_queries():
    out = np.zeros((2, EDGE_SLOTS, 48), np.float32)
    for edge in range(2):
        for r in range(6):
            for c in range(HALF):
                out[edge, r * HALF + c, r * 8 + c + (2 if edge == 1 else 0)] = 1
    return out


def pack_pair(low, high):
    return (
        low[..., :128],
        high[..., :128],
        jnp.concatenate([low[..., 128:], high[..., 128:]], axis=-1),
    )


def unpack_pair(a, b, rest):
    low = jnp.concatenate([a, rest[..., :64]], axis=-1)
    high = jnp.concatenate([b, rest[..., 64:]], axis=-1)
    return low, high


def fetch(sems, *pairs):
    copies = [pltpu.make_async_copy(source, target, sems.at[k]) for k, (source, target) in enumerate(pairs)]
    for copy in copies:
        copy.start()
    return copies


def wait_all(copies):
    for copy in copies:
        copy.wait()


def levels_of(w):
    return 2 * w + 1, (2 * w + 2) % 8


ANY = pl.BlockSpec(memory_space=pl.ANY)
VMEM = pl.BlockSpec(memory_space=pltpu.VMEM)
SMEM = pl.BlockSpec(memory_space=pltpu.SMEM)


def pack_kernel(odd_ref, field_ref, types_ref, region_ref, near_ref, far_ref, west_ref, east_ref, meta_ref):
    odd = odd_ref[0]
    lane = lax.broadcasted_iota(jnp.int32, (8, 128), 1)
    types = jnp.concatenate([types_ref[...], jnp.zeros((4, 1), jnp.int32)], axis=0)
    region = jnp.concatenate([region_ref[...], jnp.zeros((8, 128 - WLAT), jnp.int32)], axis=1)
    meta_ref[...] = jnp.where(lane == WLAT, types, region)
    near, far = pl.ds(ROWS * (1 - odd), ROWS), pl.ds(ROWS * odd, ROWS)
    cuts = (
        (near_ref, near, slice(0, 48)),
        (far_ref, far, slice(0, 48)),
        (west_ref, slice(0, 6), slice(0, HALF)),
        (east_ref, slice(0, 6), slice(48 - HALF, 48)),
    )
    for w in range(4):
        low, high = levels_of(w)
        for out, rows, columns in cuts:
            for k, part in enumerate(pack_pair(field_ref[low, rows, columns], field_ref[high, rows, columns])):
                out[w, k] = part


def pack(odd, field, types, region):
    strip, halo = (4, 3, ROWS, 48, 128), (4, 3, 6, HALF, 128)
    return pl.pallas_call(
        pack_kernel,
        in_specs=[SMEM, VMEM, VMEM, VMEM],
        out_specs=[VMEM] * 5,
        out_shape=[jax.ShapeDtypeStruct(shape, jnp.float32) for shape in (strip, strip, halo, halo)]
        + [jax.ShapeDtypeStruct((8, 128), jnp.int32)],
        compiler_params=pltpu.CompilerParams(vmem_limit_bytes=VMEM_LIMIT),
        cost_estimate=pl.CostEstimate(flops=3000000000, bytes_accessed=9000000, transcendentals=0),
        name="pack",
    )(odd, field, types, region)


def slot_lanes(slots):
    lane = lax.broadcasted_iota(jnp.int32, (8, HEADS * slots), 1)
    head, query = jnp.zeros_like(lane), lane
    for h in range(1, HEADS):
        head = jnp.where(lane >= h * slots, h, head)
        query = jnp.where(lane >= h * slots, lane - h * slots, query)
    return head, query


def slot_row(slot, rows):
    late = slot - rows * 8
    return jnp.where(late < 0, slot >> 3, ((late >> 3) << 1) + ((late >> 2) & 1))


def slot_column(slot, rows):
    return jnp.where(slot < rows * 8, slot & 7, 8 + (slot & 3))


def bias_kernel(own_ref, before_ref, table_ref, picker_ref, out_ref, edge_ref):
    bf = jnp.bfloat16
    metas = (own_ref, before_ref)

    head, query = slot_lanes(QUERIES)
    query_row = slot_row(query, 6)
    source = [slot_column(query, 6) * 48 + query_row * 8 + head]
    head, query = slot_lanes(EDGE_SLOTS)
    edge_row = jnp.zeros_like(query)
    for r in range(1, 6):
        edge_row = jnp.where(query >= r * HALF, r, edge_row)
    edge_column = query - edge_row * HALF
    for edge in range(2):
        from_row = (edge_column + (HALF if edge == 0 else 0)) * 48 + edge_row * 8 + head
        source.append(jnp.where(edge_column < HALF, from_row, -1))
    order = [
        jnp.where(lax.broadcasted_iota(jnp.int32, (WLON * 48, at.shape[1]), 0) == at[:1], 1.0, 0.0).astype(bf)
        for at in source
    ]
    key_row = slot_row(lax.broadcasted_iota(jnp.int32, (WIN, 128), 0), 12)
    out_row = lax.broadcasted_iota(jnp.int32, (64, 384), 0)
    wanted = jnp.full((64, 384), -1, jnp.int32)
    for s in range(2):
        for w in range(4):
            here = out_row >> 3 == s * 4 + w
            wanted = jnp.where(here, (out_row & 7) * 64 + metas[s][w, WLAT], wanted)
    chosen = jnp.where(lax.broadcasted_iota(jnp.int32, (64, 384), 1) == wanted, 1.0, 0.0)
    chosen = jnp.where(out_row & 7 < HEADS, chosen, 0.0).astype(bf)

    rows = jnp.dot(chosen, table_ref[...].reshape(384, BIAS_LEN), preferred_element_type=jnp.float32)
    for s in range(2):
        pieces = []
        for zi in range(WZ):
            for ai in range(ROWS):
                row = ai + ROWS * s
                begin = [(zi * WZ + zj) * WLAT * LANES + row * LANES for zj in range(WZ)]
                halves = [rows[s * 32 : (s + 1) * 32, b : b + LANES] for b in begin]
                pieces.append(jnp.concatenate(halves + [jnp.zeros((32, 384 - 2 * LANES), jnp.float32)], axis=1))
        rolled = []
        for w in range(4):
            entries = jnp.concatenate([p[w * 8 : (w + 1) * 8] for p in pieces], axis=0)
            turned = [pltpu.roll(entries, WLON - 1 - o, axis=1) for o in range(WLON - 1)] + [entries]
            rolled.append(jnp.concatenate(turned, axis=0).astype(bf))
        picked = [nt(picker_ref[s], r).astype(bf) for r in rolled]
        for w in range(4):
            bias = [jnp.dot(picked[w], o, preferred_element_type=jnp.float32) for o in order]
            key_region = jnp.zeros_like(key_row)
            query_region = jnp.zeros_like(query_row)
            edge_region = jnp.zeros_like(edge_row)
            for r in range(12):
                lev, row = 2 * w + r % 6 // ROWS, r % ROWS
                region = metas[s][lev, row + (ROWS if (r < 6) == (s == 1) else 0)]
                key_region = jnp.where(key_row == r, region, key_region)
                if r < 6:
                    query_region = jnp.where(query_row == r, region, query_region)
                    edge_region = jnp.where(edge_row == r, region, edge_region)

            def masked(values, regions):
                parts = []
                for t in range(0, regions.shape[1], 128):
                    lanes = slice(t, min(t + 128, regions.shape[1]))
                    same = key_region[:, : lanes.stop - t] == regions[:1, lanes]
                    parts.append(jnp.where(same, values[:, lanes], MASKED))
                return jnp.concatenate(parts, axis=1).astype(bf)

            out_ref[s, w] = masked(bias[0], query_region)
            for edge in range(2):
                edge_ref[s, edge, w] = masked(bias[1 + edge], edge_region)


def expand_bias(own, before, table):
    picker = jnp.asarray(key_picker()[::-1], jnp.bfloat16)
    table = table.transpose(1, 0, 2)
    shapes = ((2, 4, WIN, COLS), (2, 2, 4, WIN, EDGE_COLS))
    return pl.pallas_call(
        bias_kernel,
        in_specs=[SMEM, SMEM, VMEM, VMEM],
        out_specs=[VMEM, VMEM],
        out_shape=[jax.ShapeDtypeStruct(shape, jnp.bfloat16) for shape in shapes],
        compiler_params=pltpu.CompilerParams(vmem_limit_bytes=VMEM_LIMIT),
        cost_estimate=pl.CostEstimate(flops=6000000000, bytes_accessed=18000000, transcendentals=0),
        name="expand_bias",
    )(own, before, table, picker)


def normalize(values):
    mean = jnp.mean(values, axis=-1, keepdims=True)
    centered = values - mean
    variance = jnp.mean(centered * centered, axis=-1, keepdims=True)
    return centered * lax.rsqrt(variance + 1e-05)


def halo_tile(values):
    return jnp.concatenate([values, jnp.zeros(values.shape[:-2] + (2, C), jnp.float32)], axis=-2)


def window_tokens(grid):
    row = lax.broadcasted_iota(jnp.int32, (1, 8, C), 1)
    turn = lambda v, by: pltpu.roll(v, by, axis=1)
    own = [turn(grid[:, 8 * t : 8 * t + 8], 6) for t in range(6)]
    tiles = [None] + [jnp.where(row < 6, own[t - 1], own[t]) for t in range(1, 6)]
    low = row < 4
    windows = []
    for i in (1, 2, 3):
        base = 12 * i // 8
        first, second = tiles[base], tiles[base + 1]
        flipped = turn(second, 4)
        pairs = second.reshape(6, 2, 8, C)
        flipped_pairs = flipped.reshape(6, 2, 8, C)
        if i % 2 == 0:
            front = first
            back = jnp.where(low, pairs[:, 0], flipped_pairs[:, 1])
        else:
            front = jnp.where(low, turn(first, 4), flipped)
            back = jnp.where(low, flipped_pairs[:, 0], pairs[:, 1])
        windows.append(jnp.concatenate([front.reshape(96, C), back.reshape(48, C)], axis=0))
    return windows


def grid_tokens(windows):
    row = lax.broadcasted_iota(jnp.int32, (1, 8, C), 1)
    turn = lambda v, by: pltpu.roll(v, by, axis=1)
    low = row < 4
    tiles = [None] * 7
    for i, tokens in zip((1, 2, 3), windows):
        base = 12 * i // 8
        front, back = tokens[:48].reshape(6, 8, C), tokens[48:].reshape(3, 8, C)
        flipped = turn(back, 4)
        if i % 2 == 0:
            tiles[base] = front
            tiles[base + 1] = jnp.stack([back, flipped], axis=1).reshape(6, 8, C)
        else:
            front = turn(front, 4)
            tiles[base] = front if i == 1 else jnp.where(low, tiles[base], front)
            tiles[base + 1] = jnp.where(low, front, jnp.stack([flipped, back], axis=1).reshape(6, 8, C))
    tiles = [turn(t, 2) for t in tiles[1:6]]
    return [tiles[0]] + [jnp.where(row < 2, tiles[t - 1], tiles[t]) for t in range(1, 5)] + [tiles[4]]


def nt(a, b):
    return lax.dot_general(a, b, (((1,), (1,)), ((), ())), preferred_element_type=jnp.float32)


def eye(n):
    same = lax.broadcasted_iota(jnp.int32, (n, n), 0) == lax.broadcasted_iota(jnp.int32, (n, n), 1)
    return jnp.where(same, 1.0, 0.0).astype(jnp.bfloat16)


def split_weights(wqkv_ref, wq_ref, wk_ref, wvt_ref):
    wq_ref[...] = wqkv_ref[:, :C]
    wk_ref[...] = wqkv_ref[:, C : 2 * C]
    wvt_ref[...] = wqkv_ref[:, 2 * C :].astype(jnp.float32).T.astype(jnp.bfloat16)


def attend(queries, keys, values, bias, slots):
    bf = jnp.bfloat16
    lane = lax.broadcasted_iota(jnp.int32, (1, C), 1) // HEAD_DIM
    spread = [
        jnp.concatenate([jnp.where(lane == h, q, 0.0) for h in range(HEADS)], axis=0).astype(bf) for q in queries
    ]
    scores = [nt(k, q) for k, q in zip(keys, spread)]
    probs = []
    for s, b in zip(scores, bias):
        s = s * HEAD_DIM**-0.5 + b[...].astype(jnp.float32)
        expo = jnp.exp2((s - jnp.max(s, axis=0, keepdims=True)) * LOG2E)
        probs.append((expo * (1.0 / jnp.sum(expo, axis=0, keepdims=True))).astype(bf))
    mixed = [jnp.dot(v, p, preferred_element_type=jnp.float32) for v, p in zip(values, probs)]
    own_head = lambda m, h: m[h * HEAD_DIM : (h + 1) * HEAD_DIM, h * slots : (h + 1) * slots]
    return [jnp.concatenate([own_head(m, h) for h in range(HEADS)], axis=0).astype(bf) for m in mixed]


def feed_forward(mixed, wup_ref, wdown_ref):
    bf = jnp.bfloat16
    hidden = jax.nn.gelu(
        jnp.dot(normalize(mixed).astype(bf), wup_ref[...], preferred_element_type=jnp.float32)
    ).astype(bf)
    return mixed + nt(hidden, wdown_ref[...])


def unpack(at):
    return jnp.concatenate(unpack_pair(*[at(k) for k in range(3)]), axis=0)


def inner_kernel(odd_ref, field, strip, bias, wqkv, wproj, wup, wdown, *refs, near):
    out_ref, side, wq, wk, wvt, done, out_sems = refs[-7:]
    bf = jnp.bfloat16
    odd = odd_ref[0]
    at = 1 - odd if near else odd
    rows = pl.ds(at * ROWS, ROWS)
    split_weights(wqkv, wq, wk, wvt)
    turn = eye(QUERIES)
    sent = []
    for k in range(2):
        own = []
        for n in range(2):
            low, high = levels_of(2 * k + n)
            own.append(jnp.concatenate([field[low, rows], field[high, rows]], axis=0))
        wins = []
        for n in range(2):
            beyond = unpack(lambda part: strip[2 * k + n, part])
            wins += window_tokens(normalize(jnp.concatenate([own[n], beyond], axis=0)))
        mine = jnp.concatenate([part for t in wins for part in (t[:48], t[96:120])], axis=0).astype(bf)
        tokens = [t.astype(bf) for t in wins]
        queries = jnp.dot(mine, wq[...], preferred_element_type=jnp.float32)
        keys = jnp.dot(jnp.concatenate(tokens, axis=0), wk[...], preferred_element_type=jnp.float32).astype(bf)
        values = [nt(wvt[...], t).astype(bf) for t in tokens]
        outs = attend(
            [queries[i * QUERIES : (i + 1) * QUERIES] for i in range(6)],
            [keys[i * WIN : (i + 1) * WIN] for i in range(6)],
            values,
            [bias.at[1 - at, 2 * k + i // 3] for i in range(6)],
            QUERIES,
        )
        outs = [nt(turn, o) for o in outs]
        heads_out, residual = [], []
        for n in range(2):
            tiles = grid_tokens(outs[3 * n : 3 * n + 3])
            side[0, 2 * k + n] = tiles[0]
            side[1, 2 * k + n] = tiles[5]
            heads_out.append(jnp.concatenate(tiles[1:5], axis=1).reshape(6 * 32, C))
            residual.append(own[n][:, 8:40].reshape(6 * 32, C))
        mixed = jnp.concatenate(residual, axis=0) + jnp.dot(
            jnp.concatenate(heads_out, axis=0).astype(bf), wproj[...], preferred_element_type=jnp.float32
        )
        done[k] = feed_forward(mixed, wup, wdown).reshape(4, ROWS, 32, C)
        sent += fetch(
            out_sems.at[k],
            *[(done.at[k, n], out_ref.at[(4 * k + n + 1) % 8, rows, pl.ds(8, 32)]) for n in range(4)],
        )
    wait_all(sent)


def inner_block(near, odd, field, strip, bias, weights, so_far=None):
    operands = [odd, field, strip, bias, *weights]
    aliases = {}
    if so_far is not None:
        operands.append(so_far)
        aliases = {len(operands) - 1: 0}
    return pl.pallas_call(
        functools.partial(inner_kernel, near=near),
        in_specs=[SMEM] + [VMEM] * 7 + [ANY] * (len(operands) - 8),
        out_specs=[ANY, VMEM],
        out_shape=[
            jax.ShapeDtypeStruct(field.shape, jnp.float32),
            jax.ShapeDtypeStruct((2, 4, 6, 8, C), jnp.float32),
        ],
        scratch_shapes=[
            *[pltpu.VMEM((C, C), jnp.bfloat16)] * 3,
            pltpu.VMEM((2, 4, ROWS, 32, C), jnp.float32),
            pltpu.SemaphoreType.DMA((2, 4)),
        ],
        input_output_aliases=aliases,
        compiler_params=pltpu.CompilerParams(vmem_limit_bytes=VMEM_LIMIT),
        cost_estimate=pl.CostEstimate(flops=8000000000, bytes_accessed=24000000, transcendentals=0),
        name="near_inner" if near else "far_inner",
    )(*operands)


def edge_kernel(
    odd_ref, field, near_ref, far_ref, west_ref, east_ref, near_corner_ref, far_corner_ref, near_side_ref, far_side_ref,
    bias, gather, choose, wqkv, wproj, wup, wdown, so_far_ref, out_ref, wq, wk, wvt, done, out_sems,
):
    bf = jnp.bfloat16
    odd = odd_ref[0]
    strips, corners, sides = (near_ref, far_ref), (near_corner_ref, far_corner_ref), (near_side_ref, far_side_ref)
    halos = (west_ref, east_ref)
    columns = (pl.ds(0, 8), pl.ds(40, 8))
    split_weights(wqkv, wq, wk, wvt)
    column = lax.broadcasted_iota(jnp.int32, (1, 8, C), 1)
    sent = []
    for e in range(2):
        inner = column >= 6 if e == 0 else column < 2
        back = choose[e].astype(jnp.float32).T.astype(bf)
        for n in range(2):
            at = 1 - odd if n == 0 else odd
            rows = pl.ds(at * ROWS, ROWS)
            own, pools = [], []
            for w in range(4):
                low, high = levels_of(w)
                own.append(jnp.concatenate([field[low, rows, columns[e]], field[high, rows, columns[e]]], axis=0))
                strip = unpack(lambda k: strips[n][w, k, :, columns[e]])
                halo = halo_tile(unpack(lambda k: halos[e][w, k, rows]))
                corner = halo_tile(unpack(lambda k: corners[n][e, w, k]))
                pools.append(normalize(jnp.concatenate([own[w], strip, halo, corner], axis=0)).reshape(192, C).astype(bf))
            tokens = [jnp.dot(gather[e], p, preferred_element_type=jnp.float32).astype(bf) for p in pools]
            mine = [jnp.dot(choose[e], p[:48], preferred_element_type=jnp.float32).astype(bf) for p in pools]
            queries = jnp.dot(jnp.concatenate(mine, axis=0), wq[...], preferred_element_type=jnp.float32)
            keys = jnp.dot(jnp.concatenate(tokens, axis=0), wk[...], preferred_element_type=jnp.float32).astype(bf)
            values = [nt(wvt[...], t).astype(bf) for t in tokens]
            outs = attend(
                [queries[w * EDGE_SLOTS : (w + 1) * EDGE_SLOTS] for w in range(4)],
                [keys[w * WIN : (w + 1) * WIN] for w in range(4)],
                values,
                [bias.at[1 - at, e, w] for w in range(4)],
                EDGE_SLOTS,
            )
            placed = [nt(back, o).reshape(6, 8, C) for o in outs]
            heads_out = [jnp.where(inner, sides[n][e, w], placed[w]).reshape(48, C) for w in range(4)]
            mixed = jnp.concatenate([o.reshape(48, C) for o in own], axis=0) + jnp.dot(
                jnp.concatenate(heads_out, axis=0).astype(bf), wproj[...], preferred_element_type=jnp.float32
            )
            result = feed_forward(mixed, wup, wdown).reshape(4, 2, ROWS, 8, C)
            for w in range(4):
                low, high = levels_of(w)
                done[e, low, rows] = result[w, 0]
                done[e, high, rows] = result[w, 1]
        sent += fetch(out_sems.at[e], (done.at[e], out_ref.at[:, :, columns[e]]))
    wait_all(sent)


def edge_block(odd, field, near, far, west, east, near_corners, far_corners, near_side, far_side, bias, weights, so_far):
    gather = jnp.asarray(edge_keys(), jnp.bfloat16)
    choose = jnp.asarray(edge_queries(), jnp.bfloat16)
    operands = [
        odd, field, near, far, west, east, near_corners, far_corners, near_side, far_side, bias, gather, choose,
        *weights, so_far,
    ]
    return pl.pallas_call(
        edge_kernel,
        in_specs=[SMEM] + [VMEM] * (len(operands) - 2) + [ANY],
        out_specs=ANY,
        out_shape=jax.ShapeDtypeStruct(field.shape, jnp.float32),
        scratch_shapes=[pltpu.VMEM((C, C), jnp.bfloat16)] * 3
        + [pltpu.VMEM((2, 8, 6, 8, C), jnp.float32), pltpu.SemaphoreType.DMA((2, 1))],
        input_output_aliases={len(operands) - 1: 0},
        compiler_params=pltpu.CompilerParams(vmem_limit_bytes=VMEM_LIMIT),
        cost_estimate=pl.CostEstimate(flops=6000000000, bytes_accessed=18000000, transcendentals=0),
        name="edges",
    )(*operands)


def per_device(field, w_qkv, w_proj, w_up, w_down, bias_table, window_type, region_id):
    lats, lons = lax.axis_size("lat"), lax.axis_size("lon")
    odd = lax.rem(lax.axis_index("lat"), 2).astype(jnp.int32)
    near_route = [(i, i ^ 1) for i in range(lats)]
    far_route = [(i, (i + (1 if i % 2 else -1)) % lats) for i in range(lats)]

    near_own, far_own, to_west, to_east, meta = pack(odd.reshape(1), field, window_type, region_id)
    before = lax.ppermute(meta, "lat", [(i, (i + 1) % lats) for i in range(lats)])
    near = lax.ppermute(near_own, "lat", near_route)
    east = lax.ppermute(to_west, "lon", [(i, (i - 1) % lons) for i in range(lons)])
    west = lax.ppermute(to_east, "lon", [(i, (i + 1) % lons) for i in range(lons)])
    far = lax.ppermute(far_own, "lat", far_route)
    bias, edge_bias = expand_bias(meta, before, bias_table)
    weights = (w_qkv, w_proj, w_up, w_down.T)
    core = odd.reshape(1)
    out, near_side = inner_block(True, core, field, near, bias, weights)

    west, east, out = lax.optimization_barrier((west, east, out))
    near_at, far_at = (1 - odd) * ROWS, odd * ROWS
    cut = lambda halo, at: lax.dynamic_slice_in_dim(halo, at, ROWS, axis=2)
    near_corners = lax.ppermute(jnp.stack([cut(west, near_at), cut(east, near_at)]), "lat", near_route)
    far_corners = lax.ppermute(jnp.stack([cut(west, far_at), cut(east, far_at)]), "lat", far_route)
    out, far_side = inner_block(False, core, field, far, bias, weights, out)
    return edge_block(
        core, field, near, far, west, east, near_corners, far_corners, near_side, far_side, edge_bias, weights, out
    )


def solution(mesh):
    in_specs = (
        P(None, "lat", "lon", None),
        P(),
        P(),
        P(),
        P(),
        P(),
        P(None, "lat"),
        P(None, "lat"),
    )
    out_specs = P(None, "lat", "lon", None)
    return jax.shard_map(
        per_device, mesh=mesh, in_specs=in_specs, out_specs=out_specs, check_vma=False
    )
```

```python
import functools

import jax
import jax.numpy as jnp
from jax import lax
from jax.experimental import pallas as pl
from jax.experimental.pallas import tpu as pltpu
from jax.sharding import PartitionSpec as P

C = 192
HEADS = 6
WZ = 2
WLAT = 6
WLON = 12
HALF = 6
ROWS = 3
HEAD_DIM = 32
WIN = 144
BIAS_LEN = 3312
SPAN = 2 * WLON - 1
LANES = WLAT * SPAN
QUERIES = 72
COLS = HEADS * QUERIES
EDGE_SLOTS = 40
EDGE_COLS = HEADS * EDGE_SLOTS
LOG2E = 1.4426950408889634
MASKED = -1e30
VMEM_LIMIT = 24 * 1024 * 1024


def one_hot(at, width):
    wide = lax.broadcasted_iota(jnp.int32, (at.shape[0], width), 1)
    return jnp.where(wide == at[:, :1], 1.0, 0.0).astype(jnp.bfloat16)


def key_places():
    slot = lax.broadcasted_iota(jnp.int32, (WIN, 128), 0)
    return slot_row(slot, 12), slot_column(slot, 12)


def key_picker(upper):
    row, column = key_places()
    beyond = jnp.where(row >= 6, 1, 0)
    row = row - 6 * beyond
    level = jnp.where(row >= ROWS, 1, 0)
    row = row - ROWS * level + ROWS * (beyond if upper else 1 - beyond)
    return one_hot(level * LANES + row * SPAN + 22 - column, 384)


def edge_keys(edge):
    row, column = key_places()
    late = jnp.where(column >= HALF, 1, 0)
    mine = late if edge == 0 else 1 - late
    return one_hot(96 * (1 - mine) + row * 8 + column - HALF * late + (2 * mine if edge == 1 else 0), 192)


def edge_queries(edge):
    query = lax.broadcasted_iota(jnp.int32, (EDGE_SLOTS, 128), 0)
    row = jnp.zeros_like(query)
    for r in range(1, 6):
        row = jnp.where(query >= r * HALF, r, row)
    column = query - row * HALF
    return one_hot(jnp.where(column < HALF, row * 8 + column + (2 if edge == 1 else 0), -1), 48)


def pack_pair(low, high):
    return (
        low[..., :128],
        high[..., :128],
        jnp.concatenate([low[..., 128:], high[..., 128:]], axis=-1),
    )


def unpack_pair(a, b, rest):
    low = jnp.concatenate([a, rest[..., :64]], axis=-1)
    high = jnp.concatenate([b, rest[..., 64:]], axis=-1)
    return low, high


def fetch(sems, *pairs):
    copies = [pltpu.make_async_copy(source, target, sems.at[k]) for k, (source, target) in enumerate(pairs)]
    for copy in copies:
        copy.start()
    return copies


def wait_all(copies):
    for copy in copies:
        copy.wait()


def levels_of(w):
    return 2 * w + 1, (2 * w + 2) % 8


ANY = pl.BlockSpec(memory_space=pl.ANY)
VMEM = pl.BlockSpec(memory_space=pltpu.VMEM)


def is_odd():
    return lax.rem(lax.axis_index("lat"), 2)


def pack_kernel(field_ref, types_ref, region_ref, far_ref, near_ref, west_ref, east_ref, meta_ref, field, types, region, sems):
    order = [level for w in range(4) for level in levels_of(w)]
    small = [(types_ref, types), (region_ref, region)]
    copies = fetch(sems, *[(field_ref.at[level], field.at[level]) for level in order], *small)
    wait_all(copies[8:])
    lane = lax.broadcasted_iota(jnp.int32, (8, 128), 1)
    types = jnp.concatenate(
        [jnp.zeros((1, 8), jnp.int32), types[...], jnp.zeros((1, 116), jnp.int32)], axis=1
    )
    region = jnp.concatenate([region[...], jnp.zeros((8, 128 - WLAT), jnp.int32)], axis=1)
    meta_ref[...] = jnp.where(lane < 8, region, types)
    odd = is_odd()
    cuts = (
        (far_ref, pl.ds(ROWS * odd, ROWS), slice(0, 48)),
        (near_ref, pl.ds(ROWS * (1 - odd), ROWS), slice(0, 48)),
        (west_ref, slice(0, 6), slice(0, HALF)),
        (east_ref, slice(0, 6), slice(48 - HALF, 48)),
    )
    for w in range(4):
        wait_all(copies[2 * w : 2 * w + 2])
        low, high = levels_of(w)
        for out, rows, columns in cuts:
            for k, part in enumerate(pack_pair(field[low, rows, columns], field[high, rows, columns])):
                out[w, k] = part


def pack(field, types, region):
    strip, halo = (4, 3, ROWS, 48, 128), (4, 3, 6, HALF, 128)
    return pl.pallas_call(
        pack_kernel,
        in_specs=[ANY] * 3,
        out_specs=[VMEM] * 5,
        out_shape=[jax.ShapeDtypeStruct(shape, jnp.float32) for shape in (strip, strip, halo, halo)]
        + [jax.ShapeDtypeStruct((8, 128), jnp.int32)],
        scratch_shapes=[
            pltpu.VMEM(field.shape, jnp.float32),
            pltpu.VMEM((1, 4), jnp.int32),
            pltpu.VMEM((8, WLAT), jnp.int32),
            pltpu.SemaphoreType.DMA((10,)),
        ],
        compiler_params=pltpu.CompilerParams(vmem_limit_bytes=59 * 1024 * 1024),
        cost_estimate=pl.CostEstimate(flops=2000000000, bytes_accessed=6000000, transcendentals=0),
        name="pack",
    )(field, types.T, region)


def slot_lanes(slots):
    lane = lax.broadcasted_iota(jnp.int32, (8, HEADS * slots), 1)
    head, query = jnp.zeros_like(lane), lane
    for h in range(1, HEADS):
        head = jnp.where(lane >= h * slots, h, head)
        query = jnp.where(lane >= h * slots, lane - h * slots, query)
    return head, query


def slot_row(slot, rows):
    late = slot - rows * 8
    return jnp.where(late < 0, slot >> 3, ((late >> 3) << 1) + ((late >> 2) & 1))


def slot_column(slot, rows):
    return jnp.where(slot < rows * 8, slot & 7, 8 + (slot & 3))


def bias_kernel(own_ref, before_ref, table_ref, out_ref, edge_ref):
    bf = jnp.bfloat16
    metas = (own_ref, before_ref)

    head, query = slot_lanes(QUERIES)
    query_row = slot_row(query, 6)
    source = [slot_column(query, 6) * 48 + query_row * 8 + head]
    head, query = slot_lanes(EDGE_SLOTS)
    edge_row = jnp.zeros_like(query)
    for r in range(1, 6):
        edge_row = jnp.where(query >= r * HALF, r, edge_row)
    edge_column = query - edge_row * HALF
    for edge in range(2):
        from_row = (edge_column + (HALF if edge == 0 else 0)) * 48 + edge_row * 8 + head
        source.append(jnp.where(edge_column < HALF, from_row, -1))
    order = [
        jnp.where(lax.broadcasted_iota(jnp.int32, (WLON * 48, at.shape[1]), 0) == at[:1], 1.0, 0.0).astype(bf)
        for at in source
    ]
    key_row = slot_row(lax.broadcasted_iota(jnp.int32, (WIN, 128), 0), 12)
    out_row = lax.broadcasted_iota(jnp.int32, (64, 384), 0)
    wanted = jnp.full((64, 384), -1, jnp.int32)
    for s in range(2):
        for w in range(4):
            here = out_row >> 3 == s * 4 + w
            wanted = jnp.where(here, (out_row & 7) * 64 + metas[s][:1, 8 + w : 9 + w], wanted)
    chosen = jnp.where(lax.broadcasted_iota(jnp.int32, (64, 384), 1) == wanted, 1.0, 0.0)
    chosen = jnp.where(out_row & 7 < HEADS, chosen, 0.0).astype(bf)

    rows = jnp.dot(chosen, table_ref[...].reshape(384, BIAS_LEN), preferred_element_type=jnp.float32)
    for s in range(2):
        pieces = []
        for zi in range(WZ):
            for ai in range(ROWS):
                row = ai + ROWS * s
                begin = [(zi * WZ + zj) * WLAT * LANES + row * LANES for zj in range(WZ)]
                halves = [rows[s * 32 : (s + 1) * 32, b : b + LANES] for b in begin]
                pieces.append(jnp.concatenate(halves + [jnp.zeros((32, 384 - 2 * LANES), jnp.float32)], axis=1))
        rolled = []
        for w in range(4):
            entries = jnp.concatenate([p[w * 8 : (w + 1) * 8] for p in pieces], axis=0)
            turned = [pltpu.roll(entries, WLON - 1 - o, axis=1) for o in range(WLON - 1)] + [entries]
            rolled.append(jnp.concatenate(turned, axis=0).astype(bf))
        picker = key_picker(s == 0)
        picked = [nt(picker, r).astype(bf) for r in rolled]
        for w in range(4):
            bias = [jnp.dot(picked[w], o, preferred_element_type=jnp.float32) for o in order]
            key_region = jnp.zeros_like(key_row)
            query_region = jnp.zeros_like(query_row)
            edge_region = jnp.zeros_like(edge_row)
            for r in range(12):
                lev, row = 2 * w + r % 6 // ROWS, r % ROWS
                row += ROWS if (r < 6) == (s == 1) else 0
                region = metas[s][lev : lev + 1, row : row + 1]
                key_region = jnp.where(key_row == r, region, key_region)
                if r < 6:
                    query_region = jnp.where(query_row == r, region, query_region)
                    edge_region = jnp.where(edge_row == r, region, edge_region)

            def masked(values, regions):
                parts = []
                for t in range(0, regions.shape[1], 128):
                    lanes = slice(t, min(t + 128, regions.shape[1]))
                    same = key_region[:, : lanes.stop - t] == regions[:1, lanes]
                    parts.append(jnp.where(same, values[:, lanes], MASKED))
                return jnp.concatenate(parts, axis=1).astype(bf)

            out_ref[s, w] = masked(bias[0], query_region)
            for edge in range(2):
                edge_ref[s, edge, w] = masked(bias[1 + edge], edge_region)


def expand_bias(own, before, table):
    table = table.transpose(1, 0, 2)
    shapes = ((2, 4, WIN, COLS), (2, 2, 4, WIN, EDGE_COLS))
    return pl.pallas_call(
        bias_kernel,
        in_specs=[VMEM, VMEM, VMEM],
        out_specs=[VMEM, VMEM],
        out_shape=[jax.ShapeDtypeStruct(shape, jnp.bfloat16) for shape in shapes],
        compiler_params=pltpu.CompilerParams(vmem_limit_bytes=VMEM_LIMIT),
        cost_estimate=pl.CostEstimate(flops=6000000000, bytes_accessed=18000000, transcendentals=0),
        name="expand_bias",
    )(own, before, table)


def normalize(values):
    mean = jnp.mean(values, axis=-1, keepdims=True)
    centered = values - mean
    variance = jnp.mean(centered * centered, axis=-1, keepdims=True)
    return centered * lax.rsqrt(variance + 1e-05)


def halo_tile(values):
    return jnp.concatenate([values, jnp.zeros(values.shape[:-2] + (2, C), jnp.float32)], axis=-2)


def window_tokens(grid):
    row = lax.broadcasted_iota(jnp.int32, (1, 8, C), 1)
    turn = lambda v, by: pltpu.roll(v, by, axis=1)
    own = [turn(grid[:, 8 * t : 8 * t + 8], 6) for t in range(6)]
    tiles = [None] + [jnp.where(row < 6, own[t - 1], own[t]) for t in range(1, 6)]
    low = row < 4
    windows = []
    for i in (1, 2, 3):
        base = 12 * i // 8
        first, second = tiles[base], tiles[base + 1]
        flipped = turn(second, 4)
        pairs = second.reshape(6, 2, 8, C)
        flipped_pairs = flipped.reshape(6, 2, 8, C)
        if i % 2 == 0:
            front = first
            back = jnp.where(low, pairs[:, 0], flipped_pairs[:, 1])
        else:
            front = jnp.where(low, turn(first, 4), flipped)
            back = jnp.where(low, flipped_pairs[:, 0], pairs[:, 1])
        windows.append(jnp.concatenate([front.reshape(96, C), back.reshape(48, C)], axis=0))
    return windows


def grid_tokens(windows):
    row = lax.broadcasted_iota(jnp.int32, (1, 8, C), 1)
    turn = lambda v, by: pltpu.roll(v, by, axis=1)
    low = row < 4
    tiles = [None] * 7
    for i, tokens in zip((1, 2, 3), windows):
        base = 12 * i // 8
        front, back = tokens[:48].reshape(6, 8, C), tokens[48:].reshape(3, 8, C)
        flipped = turn(back, 4)
        if i % 2 == 0:
            tiles[base] = front
            tiles[base + 1] = jnp.stack([back, flipped], axis=1).reshape(6, 8, C)
        else:
            front = turn(front, 4)
            tiles[base] = front if i == 1 else jnp.where(low, tiles[base], front)
            tiles[base + 1] = jnp.where(low, front, jnp.stack([flipped, back], axis=1).reshape(6, 8, C))
    tiles = [turn(t, 2) for t in tiles[1:6]]
    return [tiles[0]] + [jnp.where(row < 2, tiles[t - 1], tiles[t]) for t in range(1, 5)] + [tiles[4]]


def nt(a, b):
    return lax.dot_general(a, b, (((1,), (1,)), ((), ())), preferred_element_type=jnp.float32)


def eye(n):
    same = lax.broadcasted_iota(jnp.int32, (n, n), 0) == lax.broadcasted_iota(jnp.int32, (n, n), 1)
    return jnp.where(same, 1.0, 0.0).astype(jnp.bfloat16)


def split_weights(wqkv_ref, wq_ref, wk_ref, wvt_ref):
    wq_ref[...] = wqkv_ref[:, :C]
    wk_ref[...] = wqkv_ref[:, C : 2 * C]
    wvt_ref[...] = wqkv_ref[:, 2 * C :].astype(jnp.float32).T.astype(jnp.bfloat16)


def attend(queries, keys, values, bias, slots):
    bf = jnp.bfloat16
    lane = lax.broadcasted_iota(jnp.int32, (1, C), 1) // HEAD_DIM
    spread = [
        jnp.concatenate([jnp.where(lane == h, q, 0.0) for h in range(HEADS)], axis=0).astype(bf) for q in queries
    ]
    scores = [nt(k, q) for k, q in zip(keys, spread)]
    probs = []
    for s, b in zip(scores, bias):
        s = s * HEAD_DIM**-0.5 + b[...].astype(jnp.float32)
        expo = jnp.exp2((s - jnp.max(s, axis=0, keepdims=True)) * LOG2E)
        probs.append((expo * (1.0 / jnp.sum(expo, axis=0, keepdims=True))).astype(bf))
    mixed = [jnp.dot(v, p, preferred_element_type=jnp.float32) for v, p in zip(values, probs)]
    own_head = lambda m, h: m[h * HEAD_DIM : (h + 1) * HEAD_DIM, h * slots : (h + 1) * slots]
    return [jnp.concatenate([own_head(m, h) for h in range(HEADS)], axis=0).astype(bf) for m in mixed]


def feed_forward(mixed, wup_ref, wdown_ref):
    bf = jnp.bfloat16
    hidden = jax.nn.gelu(
        jnp.dot(normalize(mixed).astype(bf), wup_ref[...], preferred_element_type=jnp.float32)
    ).astype(bf)
    return mixed + nt(hidden, wdown_ref[...])


def unpack(at):
    return jnp.concatenate(unpack_pair(*[at(k) for k in range(3)]), axis=0)


def inner_kernel(field, strip, bias, wqkv, wproj, wup, wdown, *refs, near):
    out_ref, side, wq, wk, wvt, done, out_sems = refs[-7:]
    bf = jnp.bfloat16
    odd = is_odd()
    at = 1 - odd if near else odd
    rows = pl.ds(at * ROWS, ROWS)
    split_weights(wqkv, wq, wk, wvt)
    turn = eye(QUERIES)
    sent = []
    for k in range(2):
        own = []
        for n in range(2):
            low, high = levels_of(2 * k + n)
            own.append(jnp.concatenate([field[low, rows], field[high, rows]], axis=0))
        wins = []
        for n in range(2):
            beyond = unpack(lambda part: strip[2 * k + n, part])
            wins += window_tokens(normalize(jnp.concatenate([own[n], beyond], axis=0)))
        mine = jnp.concatenate([part for t in wins for part in (t[:48], t[96:120])], axis=0).astype(bf)
        tokens = [t.astype(bf) for t in wins]
        queries = jnp.dot(mine, wq[...], preferred_element_type=jnp.float32)
        keys = jnp.dot(jnp.concatenate(tokens, axis=0), wk[...], preferred_element_type=jnp.float32).astype(bf)
        values = [nt(wvt[...], t).astype(bf) for t in tokens]
        outs = attend(
            [queries[i * QUERIES : (i + 1) * QUERIES] for i in range(6)],
            [keys[i * WIN : (i + 1) * WIN] for i in range(6)],
            values,
            [bias.at[1 - at, 2 * k + i // 3] for i in range(6)],
            QUERIES,
        )
        outs = [nt(turn, o) for o in outs]
        heads_out, residual = [], []
        for n in range(2):
            tiles = grid_tokens(outs[3 * n : 3 * n + 3])
            side[0, 2 * k + n] = tiles[0]
            side[1, 2 * k + n] = tiles[5]
            heads_out.append(jnp.concatenate(tiles[1:5], axis=1).reshape(6 * 32, C))
            residual.append(own[n][:, 8:40].reshape(6 * 32, C))
        mixed = jnp.concatenate(residual, axis=0) + jnp.dot(
            jnp.concatenate(heads_out, axis=0).astype(bf), wproj[...], preferred_element_type=jnp.float32
        )
        done[k] = feed_forward(mixed, wup, wdown).reshape(4, ROWS, 32, C)
        sent += fetch(
            out_sems.at[k],
            *[(done.at[k, n], out_ref.at[(4 * k + n + 1) % 8, rows, pl.ds(8, 32)]) for n in range(4)],
        )
    wait_all(sent)


def inner_block(near, field, strip, bias, weights, so_far=None):
    operands = [field, strip, bias, *weights]
    aliases = {}
    if so_far is not None:
        operands.append(so_far)
        aliases = {len(operands) - 1: 0}
    return pl.pallas_call(
        functools.partial(inner_kernel, near=near),
        in_specs=[VMEM] * 7 + [ANY] * (len(operands) - 7),
        out_specs=[ANY, VMEM],
        out_shape=[
            jax.ShapeDtypeStruct(field.shape, jnp.float32),
            jax.ShapeDtypeStruct((2, 4, 6, 8, C), jnp.float32),
        ],
        scratch_shapes=[
            *[pltpu.VMEM((C, C), jnp.bfloat16)] * 3,
            pltpu.VMEM((2, 4, ROWS, 32, C), jnp.float32),
            pltpu.SemaphoreType.DMA((2, 4)),
        ],
        input_output_aliases=aliases,
        compiler_params=pltpu.CompilerParams(vmem_limit_bytes=VMEM_LIMIT),
        cost_estimate=pl.CostEstimate(flops=8000000000, bytes_accessed=24000000, transcendentals=0),
        name="near_inner" if near else "far_inner",
    )(*operands)


def edge_kernel(
    field, strip_ref, west_ref, east_ref, corner_ref, side, bias, wqkv, wproj, wup, wdown, so_far_ref, out_ref,
    wq, wk, wvt, done, out_sems, *, near,
):
    bf = jnp.bfloat16
    odd = is_odd()
    at = 1 - odd if near else odd
    rows = pl.ds(at * ROWS, ROWS)
    halos = (west_ref, east_ref)
    columns = (pl.ds(0, 8), pl.ds(40, 8))
    split_weights(wqkv, wq, wk, wvt)
    column = lax.broadcasted_iota(jnp.int32, (1, 8, C), 1)
    inner = (column >= 6, column < 2)
    gather, choose = [edge_keys(e) for e in range(2)], [edge_queries(e) for e in range(2)]
    back = [c.astype(jnp.float32).T.astype(bf) for c in choose]
    units = [(e, w) for e in range(2) for w in range(4)]
    own, pools = [], []
    for e, w in units:
        low, high = levels_of(w)
        own.append(jnp.concatenate([field[low, rows, columns[e]], field[high, rows, columns[e]]], axis=0))
        strip = unpack(lambda k: strip_ref[w, k, :, columns[e]])
        halo = halo_tile(unpack(lambda k: halos[e][w, k, rows]))
        corner = halo_tile(unpack(lambda k: corner_ref[e, w, k]))
        pools.append(normalize(jnp.concatenate([own[-1], strip, halo, corner], axis=0)).reshape(192, C).astype(bf))
    matmul = lambda a, b: jnp.dot(a, b, preferred_element_type=jnp.float32)
    tokens = [matmul(gather[e], p).astype(bf) for (e, w), p in zip(units, pools)]
    mine = [matmul(choose[e], p[:48]).astype(bf) for (e, w), p in zip(units, pools)]
    queries = matmul(jnp.concatenate(mine, axis=0), wq[...])
    keys = matmul(jnp.concatenate(tokens, axis=0), wk[...]).astype(bf)
    outs = attend(
        [queries[i * EDGE_SLOTS : (i + 1) * EDGE_SLOTS] for i in range(8)],
        [keys[i * WIN : (i + 1) * WIN] for i in range(8)],
        [nt(wvt[...], t).astype(bf) for t in tokens],
        [bias.at[1 - at, e, w] for e, w in units],
        EDGE_SLOTS,
    )
    heads_out = [
        jnp.where(inner[e], side[e, w], nt(back[e], o).reshape(6, 8, C)).reshape(48, C) for (e, w), o in zip(units, outs)
    ]
    mixed = jnp.concatenate([o.reshape(48, C) for o in own], axis=0) + matmul(
        jnp.concatenate(heads_out, axis=0).astype(bf), wproj[...]
    )
    result = feed_forward(mixed, wup, wdown).reshape(8, 2, ROWS, 8, C)
    for i, (e, w) in enumerate(units):
        for n, level in enumerate(levels_of(w)):
            done[e, level] = result[i, n]
    wait_all(fetch(out_sems, *[(done.at[e], out_ref.at[:, rows, columns[e]]) for e in range(2)]))


def edge_block(near, field, strip, west, east, corners, side, bias, weights, so_far):
    operands = [field, strip, west, east, corners, side, bias, *weights, so_far]
    return pl.pallas_call(
        functools.partial(edge_kernel, near=near),
        in_specs=[VMEM] * (len(operands) - 1) + [ANY],
        out_specs=ANY,
        out_shape=jax.ShapeDtypeStruct(field.shape, jnp.float32),
        scratch_shapes=[pltpu.VMEM((C, C), jnp.bfloat16)] * 3
        + [pltpu.VMEM((2, 8, ROWS, 8, C), jnp.float32), pltpu.SemaphoreType.DMA((2,))],
        input_output_aliases={len(operands) - 1: 0},
        compiler_params=pltpu.CompilerParams(vmem_limit_bytes=VMEM_LIMIT),
        cost_estimate=pl.CostEstimate(flops=4000000000, bytes_accessed=12000000, transcendentals=0),
        name="near_edges" if near else "far_edges",
    )(*operands)


def per_device(field, w_qkv, w_proj, w_up, w_down, bias_table, window_type, region_id):
    lats, lons = lax.axis_size("lat"), lax.axis_size("lon")
    odd = lax.rem(lax.axis_index("lat"), 2).astype(jnp.int32)
    near_route = [(i, i ^ 1) for i in range(lats)]
    far_route = [(i, (i + (1 if i % 2 else -1)) % lats) for i in range(lats)]

    far_own, near_own, to_west, to_east, meta = pack(field, window_type, region_id)
    far = lax.ppermute(far_own, "lat", far_route)
    before = lax.ppermute(meta, "lat", [(i, (i + 1) % lats) for i in range(lats)])
    near = lax.ppermute(near_own, "lat", near_route)
    east = lax.ppermute(to_west, "lon", [(i, (i - 1) % lons) for i in range(lons)])
    west = lax.ppermute(to_east, "lon", [(i, (i + 1) % lons) for i in range(lons)])
    bias, edge_bias = expand_bias(meta, before, bias_table)
    weights = (w_qkv, w_proj, w_up, w_down.T)
    out, near_side = inner_block(True, field, near, bias, weights)

    west, east, out = lax.optimization_barrier((west, east, out))
    near_at, far_at = (1 - odd) * ROWS, odd * ROWS
    cut = lambda halo, at: lax.dynamic_slice_in_dim(halo, at, ROWS, axis=2)
    near_corners = lax.ppermute(jnp.stack([cut(west, near_at), cut(east, near_at)]), "lat", near_route)
    far_corners = lax.ppermute(jnp.stack([cut(west, far_at), cut(east, far_at)]), "lat", far_route)
    out = edge_block(True, field, near, west, east, near_corners, near_side, edge_bias, weights, out)
    out, far_side = inner_block(False, field, far, bias, weights, out)
    return edge_block(False, field, far, west, east, far_corners, far_side, edge_bias, weights, out)


def solution(mesh):
    in_specs = (
        P(None, "lat", "lon", None),
        P(),
        P(),
        P(),
        P(),
        P(),
        P(None, "lat"),
        P(None, "lat"),
    )
    out_specs = P(None, "lat", "lon", None)
    return jax.shard_map(
        per_device, mesh=mesh, in_specs=in_specs, out_specs=out_specs, check_vma=False
    )
```

```python
import functools

import jax
import jax.numpy as jnp
from jax import lax
from jax.experimental import pallas as pl
from jax.experimental.pallas import tpu as pltpu
from jax.sharding import PartitionSpec as P

C = 192
HEADS = 6
WZ = 2
WLAT = 6
WLON = 12
HALF = 6
ROWS = 3
HEAD_DIM = 32
WIN = 144
BIAS_LEN = 3312
SPAN = 2 * WLON - 1
LANES = WLAT * SPAN
QUERIES = 72
COLS = HEADS * QUERIES
EDGE_SLOTS = 40
EDGE_COLS = HEADS * EDGE_SLOTS
LOG2E = 1.4426950408889634
MASKED = -1e30
VMEM_LIMIT = 24 * 1024 * 1024


def one_hot(at, width):
    wide = lax.broadcasted_iota(jnp.int32, (at.shape[0], width), 1)
    return jnp.where(wide == at[:, :1], 1.0, 0.0).astype(jnp.bfloat16)


def key_places():
    slot = lax.broadcasted_iota(jnp.int32, (WIN, 128), 0)
    return slot_row(slot, 12), slot_column(slot, 12)


def key_picker(upper):
    row, column = key_places()
    beyond = jnp.where(row >= 6, 1, 0)
    row = row - 6 * beyond
    level = jnp.where(row >= ROWS, 1, 0)
    row = row - ROWS * level + ROWS * (beyond if upper else 1 - beyond)
    return one_hot(level * LANES + row * SPAN + 22 - column, 384)


def edge_keys(edge):
    row, column = key_places()
    late = jnp.where(column >= HALF, 1, 0)
    mine = late if edge == 0 else 1 - late
    return one_hot(96 * (1 - mine) + row * 8 + column - HALF * late + (2 * mine if edge == 1 else 0), 192)


def edge_queries(edge):
    query = lax.broadcasted_iota(jnp.int32, (EDGE_SLOTS, 128), 0)
    row = jnp.zeros_like(query)
    for r in range(1, 6):
        row = jnp.where(query >= r * HALF, r, row)
    column = query - row * HALF
    return one_hot(jnp.where(column < HALF, row * 8 + column + (2 if edge == 1 else 0), -1), 48)


def pack_pair(low, high):
    return (
        low[..., :128],
        high[..., :128],
        jnp.concatenate([low[..., 128:], high[..., 128:]], axis=-1),
    )


def unpack_pair(a, b, rest):
    low = jnp.concatenate([a, rest[..., :64]], axis=-1)
    high = jnp.concatenate([b, rest[..., 64:]], axis=-1)
    return low, high


def fetch(sems, *pairs):
    copies = [pltpu.make_async_copy(source, target, sems.at[k]) for k, (source, target) in enumerate(pairs)]
    for copy in copies:
        copy.start()
    return copies


def wait_all(copies):
    for copy in copies:
        copy.wait()


def levels_of(w):
    return 2 * w + 1, (2 * w + 2) % 8


ANY = pl.BlockSpec(memory_space=pl.ANY)
VMEM = pl.BlockSpec(memory_space=pltpu.VMEM)


def is_odd():
    return lax.rem(lax.axis_index("lat"), 2)


def pack_kernel(field_ref, types_ref, region_ref, far_ref, near_ref, west_ref, east_ref, meta_ref, field, types, region, sems):
    order = [level for w in range(4) for level in levels_of(w)]
    small = [(types_ref, types), (region_ref, region)]
    copies = fetch(sems, *[(field_ref.at[level], field.at[level]) for level in order], *small)
    wait_all(copies[8:])
    lane = lax.broadcasted_iota(jnp.int32, (8, 128), 1)
    types = jnp.concatenate(
        [jnp.zeros((1, 8), jnp.int32), types[...], jnp.zeros((1, 116), jnp.int32)], axis=1
    )
    region = jnp.concatenate([region[...], jnp.zeros((8, 128 - WLAT), jnp.int32)], axis=1)
    meta_ref[...] = jnp.where(lane < 8, region, types)
    odd = is_odd()
    cuts = (
        (far_ref, pl.ds(ROWS * odd, ROWS), slice(0, 48)),
        (near_ref, pl.ds(ROWS * (1 - odd), ROWS), slice(0, 48)),
        (west_ref, slice(0, 6), slice(0, HALF)),
        (east_ref, slice(0, 6), slice(48 - HALF, 48)),
    )
    for w in range(4):
        wait_all(copies[2 * w : 2 * w + 2])
        low, high = levels_of(w)
        for out, rows, columns in cuts:
            for k, part in enumerate(pack_pair(field[low, rows, columns], field[high, rows, columns])):
                out[w, k] = part


def pack(field, types, region):
    strip, halo = (4, 3, ROWS, 48, 128), (4, 3, 6, HALF, 128)
    return pl.pallas_call(
        pack_kernel,
        in_specs=[ANY] * 3,
        out_specs=[VMEM] * 5,
        out_shape=[jax.ShapeDtypeStruct(shape, jnp.float32) for shape in (strip, strip, halo, halo)]
        + [jax.ShapeDtypeStruct((8, 128), jnp.int32)],
        scratch_shapes=[
            pltpu.VMEM(field.shape, jnp.float32),
            pltpu.VMEM((1, 4), jnp.int32),
            pltpu.VMEM((8, WLAT), jnp.int32),
            pltpu.SemaphoreType.DMA((10,)),
        ],
        compiler_params=pltpu.CompilerParams(vmem_limit_bytes=59 * 1024 * 1024),
        cost_estimate=pl.CostEstimate(flops=2000000000, bytes_accessed=6000000, transcendentals=0),
        name="pack",
    )(field, types.T, region)


def slot_lanes(slots):
    lane = lax.broadcasted_iota(jnp.int32, (8, HEADS * slots), 1)
    head, query = jnp.zeros_like(lane), lane
    for h in range(1, HEADS):
        head = jnp.where(lane >= h * slots, h, head)
        query = jnp.where(lane >= h * slots, lane - h * slots, query)
    return head, query


def slot_row(slot, rows):
    late = slot - rows * 8
    return jnp.where(late < 0, slot >> 3, ((late >> 3) << 1) + ((late >> 2) & 1))


def slot_column(slot, rows):
    return jnp.where(slot < rows * 8, slot & 7, 8 + (slot & 3))


def bias_kernel(types_ref, regions_ref, before_ref, table_ref, out_ref, edge_ref):
    bf = jnp.bfloat16

    head, query = slot_lanes(QUERIES)
    query_row = slot_row(query, 6)
    source = [slot_column(query, 6) * 48 + query_row * 8 + head]
    head, query = slot_lanes(EDGE_SLOTS)
    edge_row = jnp.zeros_like(query)
    for r in range(1, 6):
        edge_row = jnp.where(query >= r * HALF, r, edge_row)
    edge_column = query - edge_row * HALF
    for edge in range(2):
        from_row = (edge_column + (HALF if edge == 0 else 0)) * 48 + edge_row * 8 + head
        source.append(jnp.where(edge_column < HALF, from_row, -1))
    order = [
        jnp.where(lax.broadcasted_iota(jnp.int32, (WLON * 48, at.shape[1]), 0) == at[:1], 1.0, 0.0).astype(bf)
        for at in source
    ]
    key_row = slot_row(lax.broadcasted_iota(jnp.int32, (WIN, 128), 0), 12)
    out_row = lax.broadcasted_iota(jnp.int32, (64, 384), 0)
    wanted = jnp.full((64, 384), -1, jnp.int32)
    for s in range(2):
        for w in range(4):
            here = out_row >> 3 == s * 4 + w
            kind = types_ref[:, w : w + 1] if s == 0 else before_ref[:1, 8 + w : 9 + w]
            wanted = jnp.where(here, (out_row & 7) * 64 + kind, wanted)
    chosen = jnp.where(lax.broadcasted_iota(jnp.int32, (64, 384), 1) == wanted, 1.0, 0.0)
    chosen = jnp.where(out_row & 7 < HEADS, chosen, 0.0).astype(bf)

    rows = jnp.dot(chosen, table_ref[...].reshape(384, BIAS_LEN), preferred_element_type=jnp.float32)
    for s in range(2):
        pieces = []
        for zi in range(WZ):
            for ai in range(ROWS):
                row = ai + ROWS * s
                begin = [(zi * WZ + zj) * WLAT * LANES + row * LANES for zj in range(WZ)]
                halves = [rows[s * 32 : (s + 1) * 32, b : b + LANES] for b in begin]
                pieces.append(jnp.concatenate(halves + [jnp.zeros((32, 384 - 2 * LANES), jnp.float32)], axis=1))
        rolled = []
        for w in range(4):
            entries = jnp.concatenate([p[w * 8 : (w + 1) * 8] for p in pieces], axis=0)
            turned = [pltpu.roll(entries, WLON - 1 - o, axis=1) for o in range(WLON - 1)] + [entries]
            rolled.append(jnp.concatenate(turned, axis=0).astype(bf))
        picker = key_picker(s == 0)
        picked = [nt(picker, r).astype(bf) for r in rolled]
        for w in range(4):
            bias = [jnp.dot(picked[w], o, preferred_element_type=jnp.float32) for o in order]
            key_region = jnp.zeros_like(key_row)
            query_region = jnp.zeros_like(query_row)
            edge_region = jnp.zeros_like(edge_row)
            for r in range(12):
                lev, row = 2 * w + r % 6 // ROWS, r % ROWS
                row += ROWS if (r < 6) == (s == 1) else 0
                region = (regions_ref, before_ref)[s][lev : lev + 1, row : row + 1]
                key_region = jnp.where(key_row == r, region, key_region)
                if r < 6:
                    query_region = jnp.where(query_row == r, region, query_region)
                    edge_region = jnp.where(edge_row == r, region, edge_region)

            def masked(values, regions):
                parts = []
                for t in range(0, regions.shape[1], 128):
                    lanes = slice(t, min(t + 128, regions.shape[1]))
                    same = key_region[:, : lanes.stop - t] == regions[:1, lanes]
                    parts.append(jnp.where(same, values[:, lanes], MASKED))
                return jnp.concatenate(parts, axis=1).astype(bf)

            out_ref[s, w] = masked(bias[0], query_region)
            for edge in range(2):
                edge_ref[s, edge, w] = masked(bias[1 + edge], edge_region)


def expand_bias(types, regions, before, table):
    table = table.transpose(1, 0, 2)
    shapes = ((2, 4, WIN, COLS), (2, 2, 4, WIN, EDGE_COLS))
    return pl.pallas_call(
        bias_kernel,
        in_specs=[VMEM] * 4,
        out_specs=[VMEM, VMEM],
        out_shape=[jax.ShapeDtypeStruct(shape, jnp.bfloat16) for shape in shapes],
        compiler_params=pltpu.CompilerParams(vmem_limit_bytes=VMEM_LIMIT),
        cost_estimate=pl.CostEstimate(flops=6000000000, bytes_accessed=18000000, transcendentals=0),
        name="expand_bias",
    )(types.T, regions, before, table)


def normalize(values):
    mean = jnp.mean(values, axis=-1, keepdims=True)
    centered = values - mean
    variance = jnp.mean(centered * centered, axis=-1, keepdims=True)
    return centered * lax.rsqrt(variance + 1e-05)


def halo_tile(values):
    return jnp.concatenate([values, jnp.zeros(values.shape[:-2] + (2, C), jnp.float32)], axis=-2)


def window_tokens(grid):
    row = lax.broadcasted_iota(jnp.int32, (1, 8, C), 1)
    turn = lambda v, by: pltpu.roll(v, by, axis=1)
    own = [turn(grid[:, 8 * t : 8 * t + 8], 6) for t in range(6)]
    tiles = [None] + [jnp.where(row < 6, own[t - 1], own[t]) for t in range(1, 6)]
    low = row < 4
    windows = []
    for i in (1, 2, 3):
        base = 12 * i // 8
        first, second = tiles[base], tiles[base + 1]
        flipped = turn(second, 4)
        pairs = second.reshape(6, 2, 8, C)
        flipped_pairs = flipped.reshape(6, 2, 8, C)
        if i % 2 == 0:
            front = first
            back = jnp.where(low, pairs[:, 0], flipped_pairs[:, 1])
        else:
            front = jnp.where(low, turn(first, 4), flipped)
            back = jnp.where(low, flipped_pairs[:, 0], pairs[:, 1])
        windows.append(jnp.concatenate([front.reshape(96, C), back.reshape(48, C)], axis=0))
    return windows


def grid_tokens(windows):
    row = lax.broadcasted_iota(jnp.int32, (1, 8, C), 1)
    turn = lambda v, by: pltpu.roll(v, by, axis=1)
    low = row < 4
    tiles = [None] * 7
    for i, tokens in zip((1, 2, 3), windows):
        base = 12 * i // 8
        front, back = tokens[:48].reshape(6, 8, C), tokens[48:].reshape(3, 8, C)
        flipped = turn(back, 4)
        if i % 2 == 0:
            tiles[base] = front
            tiles[base + 1] = jnp.stack([back, flipped], axis=1).reshape(6, 8, C)
        else:
            front = turn(front, 4)
            tiles[base] = front if i == 1 else jnp.where(low, tiles[base], front)
            tiles[base + 1] = jnp.where(low, front, jnp.stack([flipped, back], axis=1).reshape(6, 8, C))
    tiles = [turn(t, 2) for t in tiles[1:6]]
    return [tiles[0]] + [jnp.where(row < 2, tiles[t - 1], tiles[t]) for t in range(1, 5)] + [tiles[4]]


def nt(a, b):
    return lax.dot_general(a, b, (((1,), (1,)), ((), ())), preferred_element_type=jnp.float32)


def eye(n):
    same = lax.broadcasted_iota(jnp.int32, (n, n), 0) == lax.broadcasted_iota(jnp.int32, (n, n), 1)
    return jnp.where(same, 1.0, 0.0).astype(jnp.bfloat16)


def split_weights(wqkv_ref, wq_ref, wk_ref, wvt_ref):
    wq_ref[...] = wqkv_ref[:, :C]
    wk_ref[...] = wqkv_ref[:, C : 2 * C]
    wvt_ref[...] = wqkv_ref[:, 2 * C :].astype(jnp.float32).T.astype(jnp.bfloat16)


def attend(queries, keys, values, bias, slots):
    bf = jnp.bfloat16
    lane = lax.broadcasted_iota(jnp.int32, (1, C), 1) // HEAD_DIM
    spread = [
        jnp.concatenate([jnp.where(lane == h, q, 0.0) for h in range(HEADS)], axis=0).astype(bf) for q in queries
    ]
    scores = [nt(k, q) for k, q in zip(keys, spread)]
    probs = []
    for s, b in zip(scores, bias):
        s = s * HEAD_DIM**-0.5 + b[...].astype(jnp.float32)
        expo = jnp.exp2((s - jnp.max(s, axis=0, keepdims=True)) * LOG2E)
        probs.append((expo * (1.0 / jnp.sum(expo, axis=0, keepdims=True))).astype(bf))
    mixed = [jnp.dot(v, p, preferred_element_type=jnp.float32) for v, p in zip(values, probs)]
    own_head = lambda m, h: m[h * HEAD_DIM : (h + 1) * HEAD_DIM, h * slots : (h + 1) * slots]
    return [jnp.concatenate([own_head(m, h) for h in range(HEADS)], axis=0).astype(bf) for m in mixed]


def feed_forward(mixed, wup_ref, wdown_ref):
    bf = jnp.bfloat16
    hidden = jax.nn.gelu(
        jnp.dot(normalize(mixed).astype(bf), wup_ref[...], preferred_element_type=jnp.float32)
    ).astype(bf)
    return mixed + nt(hidden, wdown_ref[...])


def unpack(at):
    return jnp.concatenate(unpack_pair(*[at(k) for k in range(3)]), axis=0)


def inner_kernel(field, strip, bias, wqkv, wproj, wup, wdown, done, side, wq, wk, wvt, *, near):
    bf = jnp.bfloat16
    odd = is_odd()
    at = 1 - odd if near else odd
    rows = pl.ds(at * ROWS, ROWS)
    split_weights(wqkv, wq, wk, wvt)
    turn = eye(QUERIES)
    for k in range(2):
        own = []
        for n in range(2):
            low, high = levels_of(2 * k + n)
            own.append(jnp.concatenate([field[low, rows], field[high, rows]], axis=0))
        wins = []
        for n in range(2):
            beyond = unpack(lambda part: strip[2 * k + n, part])
            wins += window_tokens(normalize(jnp.concatenate([own[n], beyond], axis=0)))
        mine = jnp.concatenate([part for t in wins for part in (t[:48], t[96:120])], axis=0).astype(bf)
        tokens = [t.astype(bf) for t in wins]
        queries = jnp.dot(mine, wq[...], preferred_element_type=jnp.float32)
        keys = jnp.dot(jnp.concatenate(tokens, axis=0), wk[...], preferred_element_type=jnp.float32).astype(bf)
        values = [nt(wvt[...], t).astype(bf) for t in tokens]
        outs = attend(
            [queries[i * QUERIES : (i + 1) * QUERIES] for i in range(6)],
            [keys[i * WIN : (i + 1) * WIN] for i in range(6)],
            values,
            [bias.at[1 - at, 2 * k + i // 3] for i in range(6)],
            QUERIES,
        )
        outs = [nt(turn, o) for o in outs]
        heads_out, residual = [], []
        for n in range(2):
            tiles = grid_tokens(outs[3 * n : 3 * n + 3])
            side[0, 2 * k + n] = tiles[0]
            side[1, 2 * k + n] = tiles[5]
            heads_out.append(jnp.concatenate(tiles[1:5], axis=1).reshape(6 * 32, C))
            residual.append(own[n][:, 8:40].reshape(6 * 32, C))
        mixed = jnp.concatenate(residual, axis=0) + jnp.dot(
            jnp.concatenate(heads_out, axis=0).astype(bf), wproj[...], preferred_element_type=jnp.float32
        )
        done[k] = feed_forward(mixed, wup, wdown).reshape(4, ROWS, 32, C)


def inner_block(near, field, strip, bias, weights):
    return pl.pallas_call(
        functools.partial(inner_kernel, near=near),
        in_specs=[VMEM] * 7,
        out_specs=[VMEM, VMEM],
        out_shape=[
            jax.ShapeDtypeStruct((2, 4, ROWS, 32, C), jnp.float32),
            jax.ShapeDtypeStruct((2, 4, 6, 8, C), jnp.float32),
        ],
        scratch_shapes=[pltpu.VMEM((C, C), jnp.bfloat16)] * 3,
        compiler_params=pltpu.CompilerParams(vmem_limit_bytes=VMEM_LIMIT),
        cost_estimate=pl.CostEstimate(flops=8000000000, bytes_accessed=24000000, transcendentals=0),
        name="near_inner" if near else "far_inner",
    )(field, strip, bias, *weights)


def edge_kernel(
    field, strip_ref, west_ref, east_ref, corner_ref, side, bias, wqkv, wproj, wup, wdown, *refs, near,
):
    bf = jnp.bfloat16
    odd = is_odd()
    at = 1 - odd if near else odd
    rows = pl.ds(at * ROWS, ROWS)
    halos = (west_ref, east_ref)
    columns = (pl.ds(0, 8), pl.ds(40, 8))
    if near:
        done, wq, wk, wvt = refs
    else:
        near_inner_ref, far_inner_ref, near_edges_ref, out_ref, wq, wk, wvt, done, sems, last_sems = refs
        near_rows = pl.ds((1 - at) * ROWS, ROWS)
        sent = fetch(
            sems,
            *[
                (part.at[n // 4, n % 4], out_ref.at[(n + 1) % 8, part_rows, pl.ds(8, 32)])
                for part, part_rows in ((near_inner_ref, near_rows), (far_inner_ref, rows))
                for n in range(8)
            ],
            *[(near_edges_ref.at[e], out_ref.at[:, near_rows, columns[e]]) for e in range(2)],
        )
    split_weights(wqkv, wq, wk, wvt)
    column = lax.broadcasted_iota(jnp.int32, (1, 8, C), 1)
    inner = (column >= 6, column < 2)
    gather, choose = [edge_keys(e) for e in range(2)], [edge_queries(e) for e in range(2)]
    back = [c.astype(jnp.float32).T.astype(bf) for c in choose]
    units = [(e, w) for e in range(2) for w in range(4)]
    own, pools = [], []
    for e, w in units:
        low, high = levels_of(w)
        own.append(jnp.concatenate([field[low, rows, columns[e]], field[high, rows, columns[e]]], axis=0))
        strip = unpack(lambda k: strip_ref[w, k, :, columns[e]])
        halo = halo_tile(unpack(lambda k: halos[e][w, k, rows]))
        corner = halo_tile(unpack(lambda k: corner_ref[e, w, k]))
        pools.append(normalize(jnp.concatenate([own[-1], strip, halo, corner], axis=0)).reshape(192, C).astype(bf))
    matmul = lambda a, b: jnp.dot(a, b, preferred_element_type=jnp.float32)
    tokens = [matmul(gather[e], p).astype(bf) for (e, w), p in zip(units, pools)]
    mine = [matmul(choose[e], p[:48]).astype(bf) for (e, w), p in zip(units, pools)]
    queries = matmul(jnp.concatenate(mine, axis=0), wq[...])
    keys = matmul(jnp.concatenate(tokens, axis=0), wk[...]).astype(bf)
    outs = attend(
        [queries[i * EDGE_SLOTS : (i + 1) * EDGE_SLOTS] for i in range(8)],
        [keys[i * WIN : (i + 1) * WIN] for i in range(8)],
        [nt(wvt[...], t).astype(bf) for t in tokens],
        [bias.at[1 - at, e, w] for e, w in units],
        EDGE_SLOTS,
    )
    heads_out = [
        jnp.where(inner[e], side[e, w], nt(back[e], o).reshape(6, 8, C)).reshape(48, C) for (e, w), o in zip(units, outs)
    ]
    mixed = jnp.concatenate([o.reshape(48, C) for o in own], axis=0) + matmul(
        jnp.concatenate(heads_out, axis=0).astype(bf), wproj[...]
    )
    result = feed_forward(mixed, wup, wdown).reshape(8, 2, ROWS, 8, C)
    for i, (e, w) in enumerate(units):
        for n, level in enumerate(levels_of(w)):
            done[e, level] = result[i, n]
    if not near:
        wait_all(sent + fetch(last_sems, *[(done.at[e], out_ref.at[:, rows, columns[e]]) for e in range(2)]))


def edge_block(near, field, strip, west, east, corners, side, bias, weights, parts=()):
    operands = [field, strip, west, east, corners, side, bias, *weights, *parts]
    edges = (2, 8, ROWS, 8, C)
    scratch = [pltpu.VMEM((C, C), jnp.bfloat16)] * 3
    if not near:
        scratch += [
            pltpu.VMEM(edges, jnp.float32), pltpu.SemaphoreType.DMA((18,)), pltpu.SemaphoreType.DMA((2,)),
        ]
    return pl.pallas_call(
        functools.partial(edge_kernel, near=near),
        in_specs=[VMEM] * len(operands),
        out_specs=VMEM if near else ANY,
        out_shape=jax.ShapeDtypeStruct(edges if near else field.shape, jnp.float32),
        scratch_shapes=scratch,
        compiler_params=pltpu.CompilerParams(vmem_limit_bytes=VMEM_LIMIT),
        cost_estimate=pl.CostEstimate(flops=4000000000, bytes_accessed=12000000, transcendentals=0),
        name="near_edges" if near else "far_edges",
    )(*operands)


def per_device(field, w_qkv, w_proj, w_up, w_down, bias_table, window_type, region_id):
    lats, lons = lax.axis_size("lat"), lax.axis_size("lon")
    odd = lax.rem(lax.axis_index("lat"), 2).astype(jnp.int32)
    near_route = [(i, i ^ 1) for i in range(lats)]
    far_route = [(i, (i + (1 if i % 2 else -1)) % lats) for i in range(lats)]

    far_own, near_own, to_west, to_east, meta = pack(field, window_type, region_id)
    far = lax.ppermute(far_own, "lat", far_route)
    before = lax.ppermute(meta, "lat", [(i, (i + 1) % lats) for i in range(lats)])
    near = lax.ppermute(near_own, "lat", near_route)
    east = lax.ppermute(to_west, "lon", [(i, (i - 1) % lons) for i in range(lons)])
    west = lax.ppermute(to_east, "lon", [(i, (i + 1) % lons) for i in range(lons)])
    bias, edge_bias = expand_bias(window_type, region_id, before, bias_table)
    weights = (w_qkv, w_proj, w_up, w_down.T)
    near_inner, near_side = inner_block(True, field, near, bias, weights)

    west, east, near_inner = lax.optimization_barrier((west, east, near_inner))
    near_at, far_at = (1 - odd) * ROWS, odd * ROWS
    cut = lambda halo, at: lax.dynamic_slice_in_dim(halo, at, ROWS, axis=2)
    near_corners = lax.ppermute(jnp.stack([cut(west, near_at), cut(east, near_at)]), "lat", near_route)
    far_corners = lax.ppermute(jnp.stack([cut(west, far_at), cut(east, far_at)]), "lat", far_route)
    near_edges = edge_block(True, field, near, west, east, near_corners, near_side, edge_bias, weights)
    near_edges, far = lax.optimization_barrier((near_edges, far))
    far_inner, far_side = inner_block(False, field, far, bias, weights)
    parts = (near_inner, far_inner, near_edges)
    return edge_block(False, field, far, west, east, far_corners, far_side, edge_bias, weights, parts)


def solution(mesh):
    in_specs = (
        P(None, "lat", "lon", None),
        P(),
        P(),
        P(),
        P(),
        P(),
        P(None, "lat"),
        P(None, "lat"),
    )
    out_specs = P(None, "lat", "lon", None)
    return jax.shard_map(
        per_device, mesh=mesh, in_specs=in_specs, out_specs=out_specs, check_vma=False
    )
```

```python
import functools

import jax
import jax.numpy as jnp
from jax import lax
from jax.experimental import pallas as pl
from jax.experimental.pallas import tpu as pltpu
from jax.sharding import PartitionSpec as P

C = 192
HEADS = 6
WZ = 2
WLAT = 6
WLON = 12
HALF = 6
ROWS = 3
HEAD_DIM = 32
WIN = 144
BIAS_LEN = 3312
SPAN = 2 * WLON - 1
LANES = WLAT * SPAN
QUERIES = 72
GROUP = HEADS // 2 * QUERIES
EDGE_SLOTS = 40
EDGE_COLS = HEADS * EDGE_SLOTS
LOG2E = 1.4426950408889634
MASKED = -1e30
VMEM_LIMIT = 24 * 1024 * 1024


def one_hot(at, width):
    wide = lax.broadcasted_iota(jnp.int32, (at.shape[0], width), 1)
    return jnp.where(wide == at[:, :1], 1.0, 0.0).astype(jnp.bfloat16)


def key_places():
    slot = lax.broadcasted_iota(jnp.int32, (WIN, 128), 0)
    return slot_row(slot, 12), slot_column(slot, 12)


def key_picker(upper):
    row, column = key_places()
    beyond = jnp.where(row >= 6, 1, 0)
    row = row - 6 * beyond
    level = jnp.where(row >= ROWS, 1, 0)
    row = row - ROWS * level + ROWS * (beyond if upper else 1 - beyond)
    return one_hot(level * LANES + row * SPAN + 22 - column, 384)


def edge_keys(edge):
    row, column = key_places()
    late = jnp.where(column >= HALF, 1, 0)
    mine = late if edge == 0 else 1 - late
    return one_hot(96 * (1 - mine) + row * 8 + column - HALF * late + (2 * mine if edge == 1 else 0), 192)


def edge_queries(edge):
    query = lax.broadcasted_iota(jnp.int32, (EDGE_SLOTS, 128), 0)
    row = jnp.zeros_like(query)
    for r in range(1, 6):
        row = jnp.where(query >= r * HALF, r, row)
    column = query - row * HALF
    return one_hot(jnp.where(column < HALF, row * 8 + column + (2 if edge == 1 else 0), -1), 48)


def pack_pair(low, high):
    return (
        low[..., :128],
        high[..., :128],
        jnp.concatenate([low[..., 128:], high[..., 128:]], axis=-1),
    )


def unpack_pair(a, b, rest):
    low = jnp.concatenate([a, rest[..., :64]], axis=-1)
    high = jnp.concatenate([b, rest[..., 64:]], axis=-1)
    return low, high


def fetch(sems, *pairs):
    copies = [pltpu.make_async_copy(source, target, sems.at[k]) for k, (source, target) in enumerate(pairs)]
    for copy in copies:
        copy.start()
    return copies


def wait_all(copies):
    for copy in copies:
        copy.wait()


def levels_of(w):
    return 2 * w + 1, (2 * w + 2) % 8


ANY = pl.BlockSpec(memory_space=pl.ANY)
VMEM = pl.BlockSpec(memory_space=pltpu.VMEM)


def is_odd():
    return lax.rem(lax.axis_index("lat"), 2)


def pack_kernel(field_ref, types_ref, region_ref, far_ref, near_ref, west_ref, east_ref, meta_ref, field, types, region, sems):
    order = [level for w in range(4) for level in levels_of(w)]
    small = [(types_ref, types), (region_ref, region)]
    copies = fetch(sems, *[(field_ref.at[level], field.at[level]) for level in order], *small)
    wait_all(copies[8:])
    lane = lax.broadcasted_iota(jnp.int32, (8, 128), 1)
    types = jnp.concatenate(
        [jnp.zeros((1, 8), jnp.int32), types[...], jnp.zeros((1, 116), jnp.int32)], axis=1
    )
    region = jnp.concatenate([region[...], jnp.zeros((8, 128 - WLAT), jnp.int32)], axis=1)
    meta_ref[...] = jnp.where(lane < 8, region, types)
    odd = is_odd()
    cuts = (
        (far_ref, pl.ds(ROWS * odd, ROWS), slice(0, 48)),
        (near_ref, pl.ds(ROWS * (1 - odd), ROWS), slice(0, 48)),
        (west_ref, slice(0, 6), slice(0, HALF)),
        (east_ref, slice(0, 6), slice(48 - HALF, 48)),
    )
    for w in range(4):
        wait_all(copies[2 * w : 2 * w + 2])
        low, high = levels_of(w)
        for out, rows, columns in cuts:
            for k, part in enumerate(pack_pair(field[low, rows, columns], field[high, rows, columns])):
                out[w, k] = part


def pack(field, types, region):
    strip, halo = (4, 3, ROWS, 48, 128), (4, 3, 6, HALF, 128)
    return pl.pallas_call(
        pack_kernel,
        in_specs=[ANY] * 3,
        out_specs=[VMEM] * 5,
        out_shape=[jax.ShapeDtypeStruct(shape, jnp.float32) for shape in (strip, strip, halo, halo)]
        + [jax.ShapeDtypeStruct((8, 128), jnp.int32)],
        scratch_shapes=[
            pltpu.VMEM(field.shape, jnp.float32),
            pltpu.VMEM((1, 4), jnp.int32),
            pltpu.VMEM((8, WLAT), jnp.int32),
            pltpu.SemaphoreType.DMA((10,)),
        ],
        compiler_params=pltpu.CompilerParams(vmem_limit_bytes=59 * 1024 * 1024),
        cost_estimate=pl.CostEstimate(flops=2000000000, bytes_accessed=6000000, transcendentals=0),
        name="pack",
    )(field, types.T, region)


def slot_lanes(slots):
    lane = lax.broadcasted_iota(jnp.int32, (8, HEADS * slots), 1)
    head, query = jnp.zeros_like(lane), lane
    for h in range(1, HEADS):
        head = jnp.where(lane >= h * slots, h, head)
        query = jnp.where(lane >= h * slots, lane - h * slots, query)
    return head, query


def slot_row(slot, rows):
    late = slot - rows * 8
    return jnp.where(late < 0, slot >> 3, ((late >> 3) << 1) + ((late >> 2) & 1))


def slot_column(slot, rows):
    return jnp.where(slot < rows * 8, slot & 7, 8 + (slot & 3))


def bias_kernel(types_ref, regions_ref, before_ref, table_ref, out_ref, edge_ref):
    bf = jnp.bfloat16

    head, query = slot_lanes(QUERIES)
    query_row = slot_row(query, 6)
    source = slot_column(query, 6) * 48 + query_row * 8 + head
    source = [source[:, :GROUP], source[:, GROUP:]]
    query_row = [query_row[:, :GROUP], query_row[:, GROUP:]]
    head, query = slot_lanes(EDGE_SLOTS)
    edge_row = jnp.zeros_like(query)
    for r in range(1, 6):
        edge_row = jnp.where(query >= r * HALF, r, edge_row)
    edge_column = query - edge_row * HALF
    for edge in range(2):
        from_row = (edge_column + (HALF if edge == 0 else 0)) * 48 + edge_row * 8 + head
        source.append(jnp.where(edge_column < HALF, from_row, -1))
    order = [
        jnp.where(lax.broadcasted_iota(jnp.int32, (WLON * 48, at.shape[1]), 0) == at[:1], 1.0, 0.0).astype(bf)
        for at in source
    ]
    key_row = slot_row(lax.broadcasted_iota(jnp.int32, (WIN, 128), 0), 12)
    out_row = lax.broadcasted_iota(jnp.int32, (64, 384), 0)
    wanted = jnp.full((64, 384), -1, jnp.int32)
    for s in range(2):
        for w in range(4):
            here = out_row >> 3 == s * 4 + w
            kind = types_ref[:, w : w + 1] if s == 0 else before_ref[:1, 8 + w : 9 + w]
            wanted = jnp.where(here, (out_row & 7) * 64 + kind, wanted)
    chosen = jnp.where(lax.broadcasted_iota(jnp.int32, (64, 384), 1) == wanted, 1.0, 0.0)
    chosen = jnp.where(out_row & 7 < HEADS, chosen, 0.0).astype(bf)

    rows = jnp.dot(chosen, table_ref[...].reshape(384, BIAS_LEN), preferred_element_type=jnp.float32)
    for s in range(2):
        pieces = []
        for zi in range(WZ):
            for ai in range(ROWS):
                row = ai + ROWS * s
                begin = [(zi * WZ + zj) * WLAT * LANES + row * LANES for zj in range(WZ)]
                halves = [rows[s * 32 : (s + 1) * 32, b : b + LANES] for b in begin]
                pieces.append(jnp.concatenate(halves + [jnp.zeros((32, 384 - 2 * LANES), jnp.float32)], axis=1))
        rolled = []
        for w in range(4):
            entries = jnp.concatenate([p[w * 8 : (w + 1) * 8] for p in pieces], axis=0)
            turned = [pltpu.roll(entries, WLON - 1 - o, axis=1) for o in range(WLON - 1)] + [entries]
            rolled.append(jnp.concatenate(turned, axis=0).astype(bf))
        picker = key_picker(s == 0)
        picked = [nt(picker, r).astype(bf) for r in rolled]
        for w in range(4):
            bias = [jnp.dot(picked[w], o, preferred_element_type=jnp.float32) for o in order]
            key_region = jnp.zeros_like(key_row)
            query_region = [jnp.zeros_like(r) for r in query_row]
            edge_region = jnp.zeros_like(edge_row)
            for r in range(12):
                lev, row = 2 * w + r % 6 // ROWS, r % ROWS
                row += ROWS if (r < 6) == (s == 1) else 0
                region = (regions_ref, before_ref)[s][lev : lev + 1, row : row + 1]
                key_region = jnp.where(key_row == r, region, key_region)
                if r < 6:
                    query_region = [jnp.where(at == r, region, q) for at, q in zip(query_row, query_region)]
                    edge_region = jnp.where(edge_row == r, region, edge_region)

            def masked(values, regions):
                parts = []
                for t in range(0, regions.shape[1], 128):
                    lanes = slice(t, min(t + 128, regions.shape[1]))
                    same = key_region[:, : lanes.stop - t] == regions[:1, lanes]
                    parts.append(jnp.where(same, values[:, lanes], MASKED))
                return jnp.concatenate(parts, axis=1).astype(bf)

            for g in range(2):
                out_ref[s, w, g] = masked(bias[g], query_region[g])
            for edge in range(2):
                edge_ref[s, edge, w] = masked(bias[2 + edge], edge_region)


def expand_bias(types, regions, before, table):
    table = table.transpose(1, 0, 2)
    shapes = ((2, 4, 2, WIN, GROUP), (2, 2, 4, WIN, EDGE_COLS))
    return pl.pallas_call(
        bias_kernel,
        in_specs=[VMEM] * 4,
        out_specs=[VMEM, VMEM],
        out_shape=[jax.ShapeDtypeStruct(shape, jnp.bfloat16) for shape in shapes],
        compiler_params=pltpu.CompilerParams(vmem_limit_bytes=VMEM_LIMIT),
        cost_estimate=pl.CostEstimate(flops=6000000000, bytes_accessed=18000000, transcendentals=0),
        name="expand_bias",
    )(types.T, regions, before, table)


def normalize(values):
    mean = jnp.mean(values, axis=-1, keepdims=True)
    centered = values - mean
    variance = jnp.mean(centered * centered, axis=-1, keepdims=True)
    return centered * lax.rsqrt(variance + 1e-05)


def halo_tile(values):
    return jnp.concatenate([values, jnp.zeros(values.shape[:-2] + (2, C), jnp.float32)], axis=-2)


def window_tokens(grid):
    row = lax.broadcasted_iota(jnp.int32, (1, 8, C), 1)
    turn = lambda v, by: pltpu.roll(v, by, axis=1)
    own = [turn(grid[:, 8 * t : 8 * t + 8], 6) for t in range(6)]
    tiles = [None] + [jnp.where(row < 6, own[t - 1], own[t]) for t in range(1, 6)]
    low = row < 4
    windows = []
    for i in (1, 2, 3):
        base = 12 * i // 8
        first, second = tiles[base], tiles[base + 1]
        flipped = turn(second, 4)
        pairs = second.reshape(6, 2, 8, C)
        flipped_pairs = flipped.reshape(6, 2, 8, C)
        if i % 2 == 0:
            front = first
            back = jnp.where(low, pairs[:, 0], flipped_pairs[:, 1])
        else:
            front = jnp.where(low, turn(first, 4), flipped)
            back = jnp.where(low, flipped_pairs[:, 0], pairs[:, 1])
        windows.append(jnp.concatenate([front.reshape(96, C), back.reshape(48, C)], axis=0))
    return windows


def grid_tokens(windows):
    row = lax.broadcasted_iota(jnp.int32, (1, 8, C), 1)
    turn = lambda v, by: pltpu.roll(v, by, axis=1)
    low = row < 4
    tiles = [None] * 7
    for i, tokens in zip((1, 2, 3), windows):
        base = 12 * i // 8
        front, back = tokens[:48].reshape(6, 8, C), tokens[48:].reshape(3, 8, C)
        flipped = turn(back, 4)
        if i % 2 == 0:
            tiles[base] = front
            tiles[base + 1] = jnp.stack([back, flipped], axis=1).reshape(6, 8, C)
        else:
            front = turn(front, 4)
            tiles[base] = front if i == 1 else jnp.where(low, tiles[base], front)
            tiles[base + 1] = jnp.where(low, front, jnp.stack([flipped, back], axis=1).reshape(6, 8, C))
    tiles = [turn(t, 2) for t in tiles[1:6]]
    return [tiles[0]] + [jnp.where(row < 2, tiles[t - 1], tiles[t]) for t in range(1, 5)] + [tiles[4]]


def nt(a, b):
    return lax.dot_general(a, b, (((1,), (1,)), ((), ())), preferred_element_type=jnp.float32)


def eye(n):
    same = lax.broadcasted_iota(jnp.int32, (n, n), 0) == lax.broadcasted_iota(jnp.int32, (n, n), 1)
    return jnp.where(same, 1.0, 0.0).astype(jnp.bfloat16)


def split_weights(wqkv_ref, wq_ref, wk_ref, wvt_ref):
    wq_ref[...] = wqkv_ref[:, :C]
    wk_ref[...] = wqkv_ref[:, C : 2 * C]
    wvt_ref[...] = wqkv_ref[:, 2 * C :].astype(jnp.float32).T.astype(jnp.bfloat16)


def attend(queries, keys, values, bias, slots, groups):
    bf = jnp.bfloat16
    lane = lax.broadcasted_iota(jnp.int32, (1, C), 1) // HEAD_DIM
    count = HEADS // groups
    height = count * HEAD_DIM
    units = [(i, g) for i in range(len(queries)) for g in range(groups)]
    spread = [
        jnp.concatenate(
            [jnp.where(lane == h, queries[i], 0.0) for h in range(g * count, (g + 1) * count)], axis=0
        ).astype(bf)
        for i, g in units
    ]
    scores = [nt(keys[i], q) for (i, g), q in zip(units, spread)]
    probs = []
    for (i, g), s in zip(units, scores):
        s = s * HEAD_DIM**-0.5 + bias[i](g).astype(jnp.float32)
        expo = jnp.exp2((s - jnp.max(s, axis=0, keepdims=True)) * LOG2E)
        probs.append((expo * (1.0 / jnp.sum(expo, axis=0, keepdims=True))).astype(bf))
    mixed = [
        jnp.dot(values[i][g * height : (g + 1) * height], p, preferred_element_type=jnp.float32)
        for (i, g), p in zip(units, probs)
    ]
    own_head = lambda m, h: m[h * HEAD_DIM : (h + 1) * HEAD_DIM, h * slots : (h + 1) * slots]
    heads = [[own_head(m, h) for h in range(count)] for m in mixed]
    return [
        jnp.concatenate(sum(heads[i * groups : (i + 1) * groups], []), axis=0).astype(bf) for i in range(len(queries))
    ]


def feed_forward(mixed, wup_ref, wdown_ref):
    bf = jnp.bfloat16
    hidden = jax.nn.gelu(
        jnp.dot(normalize(mixed).astype(bf), wup_ref[...], preferred_element_type=jnp.float32)
    ).astype(bf)
    return mixed + nt(hidden, wdown_ref[...])


def unpack(at):
    return jnp.concatenate(unpack_pair(*[at(k) for k in range(3)]), axis=0)


def inner_kernel(field, strip, bias, wqkv, wproj, wup, wdown, done, side, wq, wk, wvt, *, near):
    bf = jnp.bfloat16
    odd = is_odd()
    at = 1 - odd if near else odd
    rows = pl.ds(at * ROWS, ROWS)
    split_weights(wqkv, wq, wk, wvt)
    turn = eye(QUERIES)
    own = []
    for n in range(4):
        low, high = levels_of(n)
        own.append(jnp.concatenate([field[low, rows], field[high, rows]], axis=0))
    wins = []
    for n in range(4):
        beyond = unpack(lambda part: strip[n, part])
        wins += window_tokens(normalize(jnp.concatenate([own[n], beyond], axis=0)))
    mine = jnp.concatenate([part for t in wins for part in (t[:48], t[96:120])], axis=0).astype(bf)
    tokens = [t.astype(bf) for t in wins]
    queries = jnp.dot(mine, wq[...], preferred_element_type=jnp.float32)
    keys = jnp.dot(jnp.concatenate(tokens, axis=0), wk[...], preferred_element_type=jnp.float32).astype(bf)
    values = [nt(wvt[...], t).astype(bf) for t in tokens]
    outs = attend(
        [queries[i * QUERIES : (i + 1) * QUERIES] for i in range(12)],
        [keys[i * WIN : (i + 1) * WIN] for i in range(12)],
        values,
        [lambda g, i=i: bias[1 - at, i // 3, g] for i in range(12)],
        QUERIES,
        2,
    )
    outs = [nt(turn, o) for o in outs]
    heads_out, residual = [], []
    for n in range(4):
        tiles = grid_tokens(outs[3 * n : 3 * n + 3])
        side[0, n] = tiles[0]
        side[1, n] = tiles[5]
        heads_out.append(jnp.concatenate(tiles[1:5], axis=1).reshape(6 * 32, C))
        residual.append(own[n][:, 8:40].reshape(6 * 32, C))
    mixed = jnp.concatenate(residual, axis=0) + jnp.dot(
        jnp.concatenate(heads_out, axis=0).astype(bf), wproj[...], preferred_element_type=jnp.float32
    )
    done[...] = feed_forward(mixed, wup, wdown).reshape(8, ROWS, 32, C)


def inner_block(near, field, strip, bias, weights):
    return pl.pallas_call(
        functools.partial(inner_kernel, near=near),
        in_specs=[VMEM] * 7,
        out_specs=[VMEM, VMEM],
        out_shape=[
            jax.ShapeDtypeStruct((8, ROWS, 32, C), jnp.float32),
            jax.ShapeDtypeStruct((2, 4, 6, 8, C), jnp.float32),
        ],
        scratch_shapes=[pltpu.VMEM((C, C), jnp.bfloat16)] * 3,
        compiler_params=pltpu.CompilerParams(vmem_limit_bytes=VMEM_LIMIT),
        cost_estimate=pl.CostEstimate(flops=8000000000, bytes_accessed=24000000, transcendentals=0),
        name="near_inner" if near else "far_inner",
    )(field, strip, bias, *weights)


def edge_kernel(
    field, strip_ref, west_ref, east_ref, corner_ref, side, bias, wqkv, wproj, wup, wdown, *refs, near,
):
    bf = jnp.bfloat16
    odd = is_odd()
    at = 1 - odd if near else odd
    rows = pl.ds(at * ROWS, ROWS)
    halos = (west_ref, east_ref)
    columns = (pl.ds(0, 8), pl.ds(40, 8))
    if near:
        done, wq, wk, wvt = refs
    else:
        near_inner_ref, far_inner_ref, near_edges_ref, out_ref, wq, wk, wvt, done, sems, last_sems = refs
        near_rows = pl.ds((1 - at) * ROWS, ROWS)
        sent = fetch(
            sems,
            *[
                (part.at[pl.ds(first, count)], out_ref.at[pl.ds((first + 1) % 8, count), part_rows, pl.ds(8, 32)])
                for part, part_rows in ((near_inner_ref, near_rows), (far_inner_ref, rows))
                for first, count in ((0, 7), (7, 1))
            ],
            *[(near_edges_ref.at[e], out_ref.at[:, near_rows, columns[e]]) for e in range(2)],
        )
    split_weights(wqkv, wq, wk, wvt)
    column = lax.broadcasted_iota(jnp.int32, (1, 8, C), 1)
    inner = (column >= 6, column < 2)
    gather, choose = [edge_keys(e) for e in range(2)], [edge_queries(e) for e in range(2)]
    back = [c.astype(jnp.float32).T.astype(bf) for c in choose]
    units = [(e, w) for e in range(2) for w in range(4)]
    own, pools = [], []
    for e, w in units:
        low, high = levels_of(w)
        own.append(jnp.concatenate([field[low, rows, columns[e]], field[high, rows, columns[e]]], axis=0))
        strip = unpack(lambda k: strip_ref[w, k, :, columns[e]])
        halo = halo_tile(unpack(lambda k: halos[e][w, k, rows]))
        corner = halo_tile(unpack(lambda k: corner_ref[e, w, k]))
        pools.append(normalize(jnp.concatenate([own[-1], strip, halo, corner], axis=0)).reshape(192, C).astype(bf))
    matmul = lambda a, b: jnp.dot(a, b, preferred_element_type=jnp.float32)
    tokens = [matmul(gather[e], p).astype(bf) for (e, w), p in zip(units, pools)]
    mine = [matmul(choose[e], p[:48]).astype(bf) for (e, w), p in zip(units, pools)]
    queries = matmul(jnp.concatenate(mine, axis=0), wq[...])
    keys = matmul(jnp.concatenate(tokens, axis=0), wk[...]).astype(bf)
    outs = attend(
        [queries[i * EDGE_SLOTS : (i + 1) * EDGE_SLOTS] for i in range(8)],
        [keys[i * WIN : (i + 1) * WIN] for i in range(8)],
        [nt(wvt[...], t).astype(bf) for t in tokens],
        [lambda g, e=e, w=w: bias[1 - at, e, w] for e, w in units],
        EDGE_SLOTS,
        1,
    )
    heads_out = [
        jnp.where(inner[e], side[e, w], nt(back[e], o).reshape(6, 8, C)).reshape(48, C) for (e, w), o in zip(units, outs)
    ]
    mixed = jnp.concatenate([o.reshape(48, C) for o in own], axis=0) + matmul(
        jnp.concatenate(heads_out, axis=0).astype(bf), wproj[...]
    )
    result = feed_forward(mixed, wup, wdown).reshape(8, 2, ROWS, 8, C)
    for i, (e, w) in enumerate(units):
        for n, level in enumerate(levels_of(w)):
            done[e, level] = result[i, n]
    if not near:
        wait_all(sent + fetch(last_sems, *[(done.at[e], out_ref.at[:, rows, columns[e]]) for e in range(2)]))


def edge_block(near, field, strip, west, east, corners, side, bias, weights, parts=()):
    operands = [field, strip, west, east, corners, side, bias, *weights, *parts]
    edges = (2, 8, ROWS, 8, C)
    scratch = [pltpu.VMEM((C, C), jnp.bfloat16)] * 3
    if not near:
        scratch += [
            pltpu.VMEM(edges, jnp.float32), pltpu.SemaphoreType.DMA((6,)), pltpu.SemaphoreType.DMA((2,)),
        ]
    return pl.pallas_call(
        functools.partial(edge_kernel, near=near),
        in_specs=[VMEM] * len(operands),
        out_specs=VMEM if near else ANY,
        out_shape=jax.ShapeDtypeStruct(edges if near else field.shape, jnp.float32),
        scratch_shapes=scratch,
        compiler_params=pltpu.CompilerParams(vmem_limit_bytes=VMEM_LIMIT),
        cost_estimate=pl.CostEstimate(flops=4000000000, bytes_accessed=12000000, transcendentals=0),
        name="near_edges" if near else "far_edges",
    )(*operands)


def per_device(field, w_qkv, w_proj, w_up, w_down, bias_table, window_type, region_id):
    lats, lons = lax.axis_size("lat"), lax.axis_size("lon")
    odd = lax.rem(lax.axis_index("lat"), 2).astype(jnp.int32)
    near_route = [(i, i ^ 1) for i in range(lats)]
    far_route = [(i, (i + (1 if i % 2 else -1)) % lats) for i in range(lats)]

    far_own, near_own, to_west, to_east, meta = pack(field, window_type, region_id)
    far = lax.ppermute(far_own, "lat", far_route)
    before = lax.ppermute(meta, "lat", [(i, (i + 1) % lats) for i in range(lats)])
    near = lax.ppermute(near_own, "lat", near_route)
    east = lax.ppermute(to_west, "lon", [(i, (i - 1) % lons) for i in range(lons)])
    west = lax.ppermute(to_east, "lon", [(i, (i + 1) % lons) for i in range(lons)])
    bias, edge_bias = expand_bias(window_type, region_id, before, bias_table)
    weights = (w_qkv, w_proj, w_up, w_down.T)
    near_inner, near_side = inner_block(True, field, near, bias, weights)

    west, east, near_inner = lax.optimization_barrier((west, east, near_inner))
    near_at, far_at = (1 - odd) * ROWS, odd * ROWS
    cut = lambda halo, at: lax.dynamic_slice_in_dim(halo, at, ROWS, axis=2)
    near_corners = lax.ppermute(jnp.stack([cut(west, near_at), cut(east, near_at)]), "lat", near_route)
    far_corners = lax.ppermute(jnp.stack([cut(west, far_at), cut(east, far_at)]), "lat", far_route)
    near_edges = edge_block(True, field, near, west, east, near_corners, near_side, edge_bias, weights)
    near_edges, far = lax.optimization_barrier((near_edges, far))
    far_inner, far_side = inner_block(False, field, far, bias, weights)
    parts = (near_inner, far_inner, near_edges)
    return edge_block(False, field, far, west, east, far_corners, far_side, edge_bias, weights, parts)


def solution(mesh):
    in_specs = (
        P(None, "lat", "lon", None),
        P(),
        P(),
        P(),
        P(),
        P(),
        P(None, "lat"),
        P(None, "lat"),
    )
    out_specs = P(None, "lat", "lon", None)
    return jax.shard_map(
        per_device, mesh=mesh, in_specs=in_specs, out_specs=out_specs, check_vma=False
    )
```

```python
import functools

import jax
import jax.numpy as jnp
from jax import lax
from jax.experimental import pallas as pl
from jax.experimental.pallas import tpu as pltpu
from jax.sharding import PartitionSpec as P

C = 192
HEADS = 6
WZ = 2
WLAT = 6
WLON = 12
HALF = 6
ROWS = 3
HEAD_DIM = 32
WIN = 144
BIAS_LEN = 3312
SPAN = 2 * WLON - 1
LANES = WLAT * SPAN
QUERIES = 72
GROUP = HEADS // 2 * QUERIES
EDGE_SLOTS = 40
EDGE_COLS = HEADS * EDGE_SLOTS
LOG2E = 1.4426950408889634
MASKED = -1e30
VMEM_LIMIT = 24 * 1024 * 1024


def one_hot(at, width):
    wide = lax.broadcasted_iota(jnp.int32, (at.shape[0], width), 1)
    return jnp.where(wide == at[:, :1], 1.0, 0.0).astype(jnp.bfloat16)


def key_places():
    slot = lax.broadcasted_iota(jnp.int32, (WIN, 128), 0)
    return slot_row(slot, 12), slot_column(slot, 12)


def key_picker(upper):
    row, column = key_places()
    beyond = jnp.where(row >= 6, 1, 0)
    row = row - 6 * beyond
    level = jnp.where(row >= ROWS, 1, 0)
    row = row - ROWS * level + ROWS * (beyond if upper else 1 - beyond)
    return one_hot(level * LANES + row * SPAN + 22 - column, 384)


def edge_keys(edge):
    row, column = key_places()
    late = jnp.where(column >= HALF, 1, 0)
    mine = late if edge == 0 else 1 - late
    return one_hot(96 * (1 - mine) + row * 8 + column - HALF * late + (2 * mine if edge == 1 else 0), 192)


def edge_queries(edge):
    query = lax.broadcasted_iota(jnp.int32, (EDGE_SLOTS, 128), 0)
    row = jnp.zeros_like(query)
    for r in range(1, 6):
        row = jnp.where(query >= r * HALF, r, row)
    column = query - row * HALF
    return one_hot(jnp.where(column < HALF, row * 8 + column + (2 if edge == 1 else 0), -1), 48)


def pack_pair(low, high):
    return (
        low[..., :128],
        high[..., :128],
        jnp.concatenate([low[..., 128:], high[..., 128:]], axis=-1),
    )


def unpack_pair(a, b, rest):
    low = jnp.concatenate([a, rest[..., :64]], axis=-1)
    high = jnp.concatenate([b, rest[..., 64:]], axis=-1)
    return low, high


def fetch(sems, *pairs):
    copies = [pltpu.make_async_copy(source, target, sems.at[k]) for k, (source, target) in enumerate(pairs)]
    for copy in copies:
        copy.start()
    return copies


def wait_all(copies):
    for copy in copies:
        copy.wait()


def levels_of(w):
    return 2 * w + 1, (2 * w + 2) % 8


ANY = pl.BlockSpec(memory_space=pl.ANY)
VMEM = pl.BlockSpec(memory_space=pltpu.VMEM)


def is_odd():
    return lax.rem(lax.axis_index("lat"), 2)


def pack_kernel(field_ref, types_ref, region_ref, far_ref, near_ref, west_ref, east_ref, meta_ref, field, types, region, sems):
    order = [level for w in range(4) for level in levels_of(w)]
    small = [(types_ref, types), (region_ref, region)]
    copies = fetch(sems, *[(field_ref.at[level], field.at[level]) for level in order], *small)
    wait_all(copies[8:])
    lane = lax.broadcasted_iota(jnp.int32, (8, 128), 1)
    types = jnp.concatenate(
        [jnp.zeros((1, 8), jnp.int32), types[...], jnp.zeros((1, 116), jnp.int32)], axis=1
    )
    region = jnp.concatenate([region[...], jnp.zeros((8, 128 - WLAT), jnp.int32)], axis=1)
    meta_ref[...] = jnp.where(lane < 8, region, types)
    odd = is_odd()
    cuts = (
        (far_ref, pl.ds(ROWS * odd, ROWS), slice(0, 48)),
        (near_ref, pl.ds(ROWS * (1 - odd), ROWS), slice(0, 48)),
        (west_ref, slice(0, 6), slice(0, HALF)),
        (east_ref, slice(0, 6), slice(48 - HALF, 48)),
    )
    for w in range(4):
        wait_all(copies[2 * w : 2 * w + 2])
        low, high = levels_of(w)
        for out, rows, columns in cuts:
            for k, part in enumerate(pack_pair(field[low, rows, columns], field[high, rows, columns])):
                out[w, k] = part


def pack(field, types, region):
    strip, halo = (4, 3, ROWS, 48, 128), (4, 3, 6, HALF, 128)
    return pl.pallas_call(
        pack_kernel,
        in_specs=[ANY] * 3,
        out_specs=[VMEM] * 5,
        out_shape=[jax.ShapeDtypeStruct(shape, jnp.float32) for shape in (strip, strip, halo, halo)]
        + [jax.ShapeDtypeStruct((8, 128), jnp.int32)],
        scratch_shapes=[
            pltpu.VMEM(field.shape, jnp.float32),
            pltpu.VMEM((1, 4), jnp.int32),
            pltpu.VMEM((8, WLAT), jnp.int32),
            pltpu.SemaphoreType.DMA((10,)),
        ],
        compiler_params=pltpu.CompilerParams(vmem_limit_bytes=59 * 1024 * 1024),
        cost_estimate=pl.CostEstimate(flops=2000000000, bytes_accessed=6000000, transcendentals=0),
        name="pack",
    )(field, types.T, region)


def slot_lanes(slots):
    lane = lax.broadcasted_iota(jnp.int32, (8, HEADS * slots), 1)
    head, query = jnp.zeros_like(lane), lane
    for h in range(1, HEADS):
        head = jnp.where(lane >= h * slots, h, head)
        query = jnp.where(lane >= h * slots, lane - h * slots, query)
    return head, query


def slot_row(slot, rows):
    late = slot - rows * 8
    return jnp.where(late < 0, slot >> 3, ((late >> 3) << 1) + ((late >> 2) & 1))


def slot_column(slot, rows):
    return jnp.where(slot < rows * 8, slot & 7, 8 + (slot & 3))


def bias_kernel(types_ref, regions_ref, before_ref, table_ref, out_ref, edge_ref):
    bf = jnp.bfloat16

    head, query = slot_lanes(QUERIES)
    query_row = slot_row(query, 6)
    source = slot_column(query, 6) * 48 + query_row * 8 + head
    source = [source[:, :GROUP], source[:, GROUP:]]
    query_row = [query_row[:, :GROUP], query_row[:, GROUP:]]
    head, query = slot_lanes(EDGE_SLOTS)
    edge_row = jnp.zeros_like(query)
    for r in range(1, 6):
        edge_row = jnp.where(query >= r * HALF, r, edge_row)
    edge_column = query - edge_row * HALF
    for edge in range(2):
        from_row = (edge_column + (HALF if edge == 0 else 0)) * 48 + edge_row * 8 + head
        source.append(jnp.where(edge_column < HALF, from_row, -1))
    order = [
        jnp.where(lax.broadcasted_iota(jnp.int32, (WLON * 48, at.shape[1]), 0) == at[:1], 1.0, 0.0).astype(bf)
        for at in source
    ]
    key_row = slot_row(lax.broadcasted_iota(jnp.int32, (WIN, 128), 0), 12)
    out_row = lax.broadcasted_iota(jnp.int32, (64, 384), 0)
    wanted = jnp.full((64, 384), -1, jnp.int32)
    for s in range(2):
        for w in range(4):
            here = out_row >> 3 == s * 4 + w
            kind = types_ref[:, w : w + 1] if s == 0 else before_ref[:1, 8 + w : 9 + w]
            wanted = jnp.where(here, (out_row & 7) * 64 + kind, wanted)
    chosen = jnp.where(lax.broadcasted_iota(jnp.int32, (64, 384), 1) == wanted, 1.0, 0.0)
    chosen = jnp.where(out_row & 7 < HEADS, chosen, 0.0).astype(bf)

    rows = jnp.dot(chosen, table_ref[...].reshape(384, BIAS_LEN), preferred_element_type=jnp.float32)
    for s in range(2):
        pieces = []
        for zi in range(WZ):
            for ai in range(ROWS):
                row = ai + ROWS * s
                begin = [(zi * WZ + zj) * WLAT * LANES + row * LANES for zj in range(WZ)]
                halves = [rows[s * 32 : (s + 1) * 32, b : b + LANES] for b in begin]
                pieces.append(jnp.concatenate(halves + [jnp.zeros((32, 384 - 2 * LANES), jnp.float32)], axis=1))
        rolled = []
        for w in range(4):
            entries = jnp.concatenate([p[w * 8 : (w + 1) * 8] for p in pieces], axis=0)
            turned = [pltpu.roll(entries, WLON - 1 - o, axis=1) for o in range(WLON - 1)] + [entries]
            rolled.append(jnp.concatenate(turned, axis=0).astype(bf))
        picker = key_picker(s == 0)
        picked = [nt(picker, r).astype(bf) for r in rolled]
        for w in range(4):
            bias = [jnp.dot(picked[w], o, preferred_element_type=jnp.float32) for o in order]
            key_region = jnp.zeros_like(key_row)
            query_region = [jnp.zeros_like(r) for r in query_row]
            edge_region = jnp.zeros_like(edge_row)
            for r in range(12):
                lev, row = 2 * w + r % 6 // ROWS, r % ROWS
                row += ROWS if (r < 6) == (s == 1) else 0
                region = (regions_ref, before_ref)[s][lev : lev + 1, row : row + 1]
                key_region = jnp.where(key_row == r, region, key_region)
                if r < 6:
                    query_region = [jnp.where(at == r, region, q) for at, q in zip(query_row, query_region)]
                    edge_region = jnp.where(edge_row == r, region, edge_region)

            def masked(values, regions):
                parts = []
                for t in range(0, regions.shape[1], 128):
                    lanes = slice(t, min(t + 128, regions.shape[1]))
                    same = key_region[:, : lanes.stop - t] == regions[:1, lanes]
                    parts.append(jnp.where(same, values[:, lanes], MASKED))
                return jnp.concatenate(parts, axis=1).astype(bf)

            for g in range(2):
                out_ref[s, w, g] = masked(bias[g], query_region[g])
            for edge in range(2):
                edge_ref[s, edge, w] = masked(bias[2 + edge], edge_region)


def expand_bias(types, regions, before, table):
    table = table.transpose(1, 0, 2)
    shapes = ((2, 4, 2, WIN, GROUP), (2, 2, 4, WIN, EDGE_COLS))
    return pl.pallas_call(
        bias_kernel,
        in_specs=[VMEM] * 4,
        out_specs=[VMEM, VMEM],
        out_shape=[jax.ShapeDtypeStruct(shape, jnp.bfloat16) for shape in shapes],
        compiler_params=pltpu.CompilerParams(vmem_limit_bytes=VMEM_LIMIT),
        cost_estimate=pl.CostEstimate(flops=6000000000, bytes_accessed=18000000, transcendentals=0),
        name="expand_bias",
    )(types.T, regions, before, table)


def normalize(values):
    mean = jnp.mean(values, axis=-1, keepdims=True)
    centered = values - mean
    variance = jnp.mean(centered * centered, axis=-1, keepdims=True)
    return centered * lax.rsqrt(variance + 1e-05)


def halo_tile(values):
    return jnp.concatenate([values, jnp.zeros(values.shape[:-2] + (2, C), jnp.float32)], axis=-2)


def window_tokens(grid):
    row = lax.broadcasted_iota(jnp.int32, (1, 8, C), 1)
    turn = lambda v, by: pltpu.roll(v, by, axis=1)
    own = [turn(grid[:, 8 * t : 8 * t + 8], 6) for t in range(6)]
    tiles = [None] + [jnp.where(row < 6, own[t - 1], own[t]) for t in range(1, 6)]
    low = row < 4
    windows = []
    for i in (1, 2, 3):
        base = 12 * i // 8
        first, second = tiles[base], tiles[base + 1]
        flipped = turn(second, 4)
        pairs = second.reshape(6, 2, 8, C)
        flipped_pairs = flipped.reshape(6, 2, 8, C)
        if i % 2 == 0:
            front = first
            back = jnp.where(low, pairs[:, 0], flipped_pairs[:, 1])
        else:
            front = jnp.where(low, turn(first, 4), flipped)
            back = jnp.where(low, flipped_pairs[:, 0], pairs[:, 1])
        windows.append(jnp.concatenate([front.reshape(96, C), back.reshape(48, C)], axis=0))
    return windows


def grid_tokens(windows):
    row = lax.broadcasted_iota(jnp.int32, (1, 8, C), 1)
    turn = lambda v, by: pltpu.roll(v, by, axis=1)
    low = row < 4
    tiles = [None] * 7
    for i, tokens in zip((1, 2, 3), windows):
        base = 12 * i // 8
        front, back = tokens[:48].reshape(6, 8, C), tokens[48:].reshape(3, 8, C)
        flipped = turn(back, 4)
        if i % 2 == 0:
            tiles[base] = front
            tiles[base + 1] = jnp.stack([back, flipped], axis=1).reshape(6, 8, C)
        else:
            front = turn(front, 4)
            tiles[base] = front if i == 1 else jnp.where(low, tiles[base], front)
            tiles[base + 1] = jnp.where(low, front, jnp.stack([flipped, back], axis=1).reshape(6, 8, C))
    tiles = [turn(t, 2) for t in tiles[1:6]]
    return [tiles[0]] + [jnp.where(row < 2, tiles[t - 1], tiles[t]) for t in range(1, 5)] + [tiles[4]]


def nt(a, b):
    return lax.dot_general(a, b, (((1,), (1,)), ((), ())), preferred_element_type=jnp.float32)


def eye(n):
    same = lax.broadcasted_iota(jnp.int32, (n, n), 0) == lax.broadcasted_iota(jnp.int32, (n, n), 1)
    return jnp.where(same, 1.0, 0.0).astype(jnp.bfloat16)


def split_weights(wqkv_ref, wq_ref, wk_ref, wvt_ref):
    wq_ref[...] = wqkv_ref[:, :C]
    wk_ref[...] = wqkv_ref[:, C : 2 * C]
    wvt_ref[...] = wqkv_ref[:, 2 * C :].astype(jnp.float32).T.astype(jnp.bfloat16)


def attend(queries, keys, values, bias, slots, groups):
    bf = jnp.bfloat16
    lane = lax.broadcasted_iota(jnp.int32, (1, C), 1) // HEAD_DIM
    count = HEADS // groups
    height = count * HEAD_DIM
    units = [(i, g) for i in range(len(queries)) for g in range(groups)]
    spread = [
        jnp.concatenate(
            [jnp.where(lane == h, queries[i], 0.0) for h in range(g * count, (g + 1) * count)], axis=0
        ).astype(bf)
        for i, g in units
    ]
    scores = [nt(keys[i], q) for (i, g), q in zip(units, spread)]
    probs, scales = [], []
    for (i, g), s in zip(units, scores):
        s = s * HEAD_DIM**-0.5 + bias[i](g).astype(jnp.float32)
        expo = jnp.exp2((s - jnp.max(s, axis=0, keepdims=True)) * LOG2E)
        probs.append(expo.astype(bf))
        scales.append(1.0 / jnp.sum(expo, axis=0, keepdims=True))
    mixed = [
        jnp.dot(values[i][g * height : (g + 1) * height], p, preferred_element_type=jnp.float32) * scale
        for (i, g), p, scale in zip(units, probs, scales)
    ]
    own_head = lambda m, h: m[h * HEAD_DIM : (h + 1) * HEAD_DIM, h * slots : (h + 1) * slots]
    heads = [[own_head(m, h) for h in range(count)] for m in mixed]
    return [
        jnp.concatenate(sum(heads[i * groups : (i + 1) * groups], []), axis=0).astype(bf) for i in range(len(queries))
    ]


def feed_forward(mixed, wup_ref, wdown_ref):
    bf = jnp.bfloat16
    hidden = jax.nn.gelu(
        jnp.dot(normalize(mixed).astype(bf), wup_ref[...], preferred_element_type=jnp.float32)
    ).astype(bf)
    return mixed + nt(hidden, wdown_ref[...])


def unpack(at):
    return jnp.concatenate(unpack_pair(*[at(k) for k in range(3)]), axis=0)


def inner_kernel(field, strip, bias, wqkv, wproj, wup, wdown, done, side, wq, wk, wvt, *, near):
    bf = jnp.bfloat16
    odd = is_odd()
    at = 1 - odd if near else odd
    rows = pl.ds(at * ROWS, ROWS)
    split_weights(wqkv, wq, wk, wvt)
    turn = eye(QUERIES)
    own = []
    for n in range(4):
        low, high = levels_of(n)
        own.append(jnp.concatenate([field[low, rows], field[high, rows]], axis=0))
    wins = []
    for n in range(4):
        beyond = unpack(lambda part: strip[n, part])
        wins += window_tokens(normalize(jnp.concatenate([own[n], beyond], axis=0)))
    mine = jnp.concatenate([part for t in wins for part in (t[:48], t[96:120])], axis=0).astype(bf)
    tokens = [t.astype(bf) for t in wins]
    queries = jnp.dot(mine, wq[...], preferred_element_type=jnp.float32)
    keys = jnp.dot(jnp.concatenate(tokens, axis=0), wk[...], preferred_element_type=jnp.float32).astype(bf)
    values = [nt(wvt[...], t).astype(bf) for t in tokens]
    outs = attend(
        [queries[i * QUERIES : (i + 1) * QUERIES] for i in range(12)],
        [keys[i * WIN : (i + 1) * WIN] for i in range(12)],
        values,
        [lambda g, i=i: bias[1 - at, i // 3, g] for i in range(12)],
        QUERIES,
        2,
    )
    outs = [nt(turn, o) for o in outs]
    heads_out, residual = [], []
    for n in range(4):
        tiles = grid_tokens(outs[3 * n : 3 * n + 3])
        side[0, n] = tiles[0]
        side[1, n] = tiles[5]
        heads_out.append(jnp.concatenate(tiles[1:5], axis=1).reshape(6 * 32, C))
        residual.append(own[n][:, 8:40].reshape(6 * 32, C))
    mixed = jnp.concatenate(residual, axis=0) + jnp.dot(
        jnp.concatenate(heads_out, axis=0).astype(bf), wproj[...], preferred_element_type=jnp.float32
    )
    done[...] = feed_forward(mixed, wup, wdown).reshape(8, ROWS, 32, C)


def inner_block(near, field, strip, bias, weights):
    return pl.pallas_call(
        functools.partial(inner_kernel, near=near),
        in_specs=[VMEM] * 7,
        out_specs=[VMEM, VMEM],
        out_shape=[
            jax.ShapeDtypeStruct((8, ROWS, 32, C), jnp.float32),
            jax.ShapeDtypeStruct((2, 4, 6, 8, C), jnp.float32),
        ],
        scratch_shapes=[pltpu.VMEM((C, C), jnp.bfloat16)] * 3,
        compiler_params=pltpu.CompilerParams(vmem_limit_bytes=VMEM_LIMIT),
        cost_estimate=pl.CostEstimate(flops=8000000000, bytes_accessed=24000000, transcendentals=0),
        name="near_inner" if near else "far_inner",
    )(field, strip, bias, *weights)


def edge_kernel(
    field, strip_ref, west_ref, east_ref, corner_ref, side, bias, wqkv, wproj, wup, wdown, *refs, near,
):
    bf = jnp.bfloat16
    odd = is_odd()
    at = 1 - odd if near else odd
    rows = pl.ds(at * ROWS, ROWS)
    halos = (west_ref, east_ref)
    columns = (pl.ds(0, 8), pl.ds(40, 8))
    if near:
        done, wq, wk, wvt = refs
    else:
        near_inner_ref, far_inner_ref, near_edges_ref, out_ref, wq, wk, wvt, done, sems, last_sems = refs
        near_rows = pl.ds((1 - at) * ROWS, ROWS)
        sent = fetch(
            sems,
            *[
                (part.at[pl.ds(first, count)], out_ref.at[pl.ds((first + 1) % 8, count), part_rows, pl.ds(8, 32)])
                for part, part_rows in ((near_inner_ref, near_rows), (far_inner_ref, rows))
                for first, count in ((0, 7), (7, 1))
            ],
            *[(near_edges_ref.at[e], out_ref.at[:, near_rows, columns[e]]) for e in range(2)],
        )
    split_weights(wqkv, wq, wk, wvt)
    column = lax.broadcasted_iota(jnp.int32, (1, 8, C), 1)
    inner = (column >= 6, column < 2)
    gather, choose = [edge_keys(e) for e in range(2)], [edge_queries(e) for e in range(2)]
    back = [c.astype(jnp.float32).T.astype(bf) for c in choose]
    units = [(e, w) for e in range(2) for w in range(4)]
    own, pools = [], []
    for e, w in units:
        low, high = levels_of(w)
        own.append(jnp.concatenate([field[low, rows, columns[e]], field[high, rows, columns[e]]], axis=0))
        strip = unpack(lambda k: strip_ref[w, k, :, columns[e]])
        halo = halo_tile(unpack(lambda k: halos[e][w, k, rows]))
        corner = halo_tile(unpack(lambda k: corner_ref[e, w, k]))
        pools.append(normalize(jnp.concatenate([own[-1], strip, halo, corner], axis=0)).reshape(192, C).astype(bf))
    matmul = lambda a, b: jnp.dot(a, b, preferred_element_type=jnp.float32)
    tokens = [matmul(gather[e], p).astype(bf) for (e, w), p in zip(units, pools)]
    mine = [matmul(choose[e], p[:48]).astype(bf) for (e, w), p in zip(units, pools)]
    queries = matmul(jnp.concatenate(mine, axis=0), wq[...])
    keys = matmul(jnp.concatenate(tokens, axis=0), wk[...]).astype(bf)
    outs = attend(
        [queries[i * EDGE_SLOTS : (i + 1) * EDGE_SLOTS] for i in range(8)],
        [keys[i * WIN : (i + 1) * WIN] for i in range(8)],
        [nt(wvt[...], t).astype(bf) for t in tokens],
        [lambda g, e=e, w=w: bias[1 - at, e, w] for e, w in units],
        EDGE_SLOTS,
        1,
    )
    heads_out = [
        jnp.where(inner[e], side[e, w], nt(back[e], o).reshape(6, 8, C)).reshape(48, C) for (e, w), o in zip(units, outs)
    ]
    mixed = jnp.concatenate([o.reshape(48, C) for o in own], axis=0) + matmul(
        jnp.concatenate(heads_out, axis=0).astype(bf), wproj[...]
    )
    result = feed_forward(mixed, wup, wdown).reshape(8, 2, ROWS, 8, C)
    for i, (e, w) in enumerate(units):
        for n, level in enumerate(levels_of(w)):
            done[e, level] = result[i, n]
    if not near:
        wait_all(sent + fetch(last_sems, *[(done.at[e], out_ref.at[:, rows, columns[e]]) for e in range(2)]))


def edge_block(near, field, strip, west, east, corners, side, bias, weights, parts=()):
    operands = [field, strip, west, east, corners, side, bias, *weights, *parts]
    edges = (2, 8, ROWS, 8, C)
    scratch = [pltpu.VMEM((C, C), jnp.bfloat16)] * 3
    if not near:
        scratch += [
            pltpu.VMEM(edges, jnp.float32), pltpu.SemaphoreType.DMA((6,)), pltpu.SemaphoreType.DMA((2,)),
        ]
    return pl.pallas_call(
        functools.partial(edge_kernel, near=near),
        in_specs=[VMEM] * len(operands),
        out_specs=VMEM if near else ANY,
        out_shape=jax.ShapeDtypeStruct(edges if near else field.shape, jnp.float32),
        scratch_shapes=scratch,
        compiler_params=pltpu.CompilerParams(vmem_limit_bytes=VMEM_LIMIT),
        cost_estimate=pl.CostEstimate(flops=4000000000, bytes_accessed=12000000, transcendentals=0),
        name="near_edges" if near else "far_edges",
    )(*operands)


def per_device(field, w_qkv, w_proj, w_up, w_down, bias_table, window_type, region_id):
    lats, lons = lax.axis_size("lat"), lax.axis_size("lon")
    odd = lax.rem(lax.axis_index("lat"), 2).astype(jnp.int32)
    near_route = [(i, i ^ 1) for i in range(lats)]
    far_route = [(i, (i + (1 if i % 2 else -1)) % lats) for i in range(lats)]

    far_own, near_own, to_west, to_east, meta = pack(field, window_type, region_id)
    far = lax.ppermute(far_own, "lat", far_route)
    before = lax.ppermute(meta, "lat", [(i, (i + 1) % lats) for i in range(lats)])
    near = lax.ppermute(near_own, "lat", near_route)
    east = lax.ppermute(to_west, "lon", [(i, (i - 1) % lons) for i in range(lons)])
    west = lax.ppermute(to_east, "lon", [(i, (i + 1) % lons) for i in range(lons)])
    bias, edge_bias = expand_bias(window_type, region_id, before, bias_table)
    weights = (w_qkv, w_proj, w_up, w_down.T)
    near_inner, near_side = inner_block(True, field, near, bias, weights)

    west, east, near_inner = lax.optimization_barrier((west, east, near_inner))
    near_at, far_at = (1 - odd) * ROWS, odd * ROWS
    cut = lambda halo, at: lax.dynamic_slice_in_dim(halo, at, ROWS, axis=2)
    near_corners = lax.ppermute(jnp.stack([cut(west, near_at), cut(east, near_at)]), "lat", near_route)
    far_corners = lax.ppermute(jnp.stack([cut(west, far_at), cut(east, far_at)]), "lat", far_route)
    near_edges = edge_block(True, field, near, west, east, near_corners, near_side, edge_bias, weights)
    near_edges, far = lax.optimization_barrier((near_edges, far))
    far_inner, far_side = inner_block(False, field, far, bias, weights)
    parts = (near_inner, far_inner, near_edges)
    return edge_block(False, field, far, west, east, far_corners, far_side, edge_bias, weights, parts)


def solution(mesh):
    in_specs = (
        P(None, "lat", "lon", None),
        P(),
        P(),
        P(),
        P(),
        P(),
        P(None, "lat"),
        P(None, "lat"),
    )
    out_specs = P(None, "lat", "lon", None)
    return jax.shard_map(
        per_device, mesh=mesh, in_specs=in_specs, out_specs=out_specs, check_vma=False
    )
```
